256 devices in a mesh: mem: 16 (over y_lo, x, core), tile: 16 (over y_hi, z).
Axes of the slice: x: 4, y: 4 (y_hi: 2, y_lo: 2; y = y_hi * 2 + y_lo), z: 8, core: 2. Of those that a mesh axis runs over, the one named last changes fastest.
Arguments:
- perturb: bfloat16 [80, 2, 2, 256, 2048], P('mem', None, None, None, 'tile'), may hold values from -6 to 6
- coef_x: float32 [2, 256, 2048], P(None, None, 'tile'), may hold values from 0.25 to 0.5
- coef_y: float32 [2, 256, 2048], P(None, None, 'tile'), may hold values from 0.25 to 0.5
- obs_values: float32 [524288], P(('mem', 'tile')), may hold values from -12 to 12
- obs_tile: int32 [524288, 1], P(('mem', 'tile')), may hold values from 0 to 15; in each aligned block of 2048 rows (0 to 2047, 2048 to 4095, ...) at most 384 rows name the same one
- obs_cell: int32 [524288], P(('mem', 'tile')), may hold values from 0 to 131071
Outputs:
- increment: float32 [256, 2, 2, 2048], P('mem', None, None, 'tile')
The draws below stay inside these ranges and needn't reach their ends.
Inputs may be any that keep to these rules, and one draw needn't show every extreme that they name: `obs_tile`: among the 2048 observations of one device no tile is named more than 384 times, and in every draw some device names some tile exactly 384 times.
All inputs are finite; a program needn't handle non-finite values.
Results may differ from the reference program's by a relative error of at most 0.0003.
Values sent between devices are 32-bit elements; how exact they have to be, the bound alone decides.
A program may use at most 64 MiB of HBM per device.

```python
import math
import jax
import jax.numpy as jnp
import numpy as np
from jax import lax

FIELDS = 2
LEVELS = 2
SWEEPS = 6
LAT = 256
LON_DEV = 128
OBS_DEV = 2048
MEMBERS = 80
TILES = 16
NLON = 2048
OBS_TOTAL = 524288
CAP = 384


def plant(values, key, low, largest):
    longest = values.shape.index(max(values.shape))
    spots = []
    for shift in (0, 1):
        where = [jax.random.randint(jax.random.fold_in(key, axis), (), 0, length) for axis, length in enumerate(values.shape)]
        where[longest] = (where[longest] + shift) % values.shape[longest]
        spots.append(tuple(where))
    return values.at[spots[0]].set(low).at[spots[1]].set(largest)


def with_spikes(values, key, source, target, blocks, factor):
    owner, partner = [(jnp.arange(values.shape[position]) // (values.shape[position] // blocks)).reshape([-1 if axis == position else 1 for axis in range(values.ndim)]) for position in (source, target)]
    chosen = jax.random.permutation(key, blocks)[partner]
    strong = (owner == chosen) | (owner == (partner + blocks // 2) % blocks)
    return jnp.where(strong, factor * values, values)


def block_levels(key, shape, shards, low, largest):
    def one(position, parts):
        heights = jax.random.uniform(jax.random.fold_in(jax.random.fold_in(key, 6), position), (parts,), jnp.float32, low / len(shards), largest / len(shards))
        return jnp.repeat(jnp.exp(heights), shape[position] // parts).reshape((-1,) + (1,) * (len(shape) - position - 1))

    gain = one(*shards[0])
    for cut in shards[1:]:
        gain = gain * one(*cut)
    return gain


def shared_out(rng, own, number, rows, number_of, top, limit, slope):
    order = jax.random.permutation(rng, number_of)
    crowded, usual = shares(number_of, rows * top, limit, slope, True), shares(number_of, rows * top, limit, slope, False)
    places = jnp.arange(number_of)

    def named(lengths, turn):
        used = int((lengths > 0).sum())
        fixed = max(1, used // 4)
        shifted = fixed + (places - fixed + turn * (used - fixed)) % max(1, number_of - fixed)
        return jnp.zeros((number_of,), jnp.int32).at[order[jnp.where(places < fixed, places, shifted)]].set(jnp.asarray(lengths, jnp.int32))

    lengths = jnp.where(number % 4 == 0, named(crowded, number // 4), named(usual, number - number // 4 - 1))
    mixed = jax.random.permutation(jax.random.fold_in(own, 3), number_of)
    source_of, taker = mixed[0:number_of // 2 * 2:2], mixed[1:number_of // 2 * 2:2]
    slack = jnp.minimum(lengths[source_of] - 1, limit - lengths[taker]) // 2
    slack = jnp.where((source_of == order[0]) | (taker == order[0]) | (lengths[taker] == 0), 0, jnp.maximum(slack, 0))
    shifted = jax.random.randint(jax.random.fold_in(own, 4), (number_of // 2,), 0, 1 << 20) % (slack + 1)
    lengths = lengths.at[source_of].add(-shifted).at[taker].add(shifted)
    items = jnp.searchsorted(jnp.cumsum(lengths), jnp.arange(rows * top), side="right").astype(jnp.int32)
    listing = items.reshape(top, rows).T
    listing = listing[jax.random.permutation(jax.random.fold_in(own, 1), rows)]
    turn = jax.random.randint(jax.random.fold_in(own, 2), (rows, 1), 0, top)
    return jnp.take_along_axis(listing, (jnp.arange(top)[None, :] + turn) % top, axis=1)


def shares(count, total, most, skew, full):
    loads = [(1 << 20) // math.isqrt(grade ** skew) + 1 for grade in range(1, count + 1)]
    largest = most if full else min(most, max(-(-total // count), total * loads[0] // sum(loads)))
    least = 1 if total - largest >= count - 1 else 0
    counts, spare = [largest] + [least] * (count - 1), total - largest - least * (count - 1)
    while spare > 0:
        movable = [i for i in range(1, count) if counts[i] < largest] or [i for i in range(1, count) if counts[i] < most]
        pool, budget = sum([loads[i] for i in movable]), spare
        for i in movable:
            extra = min(most - counts[i], max(1, budget * loads[i] // pool), spare)
            counts[i] = counts[i] + extra
            spare = spare - extra
    return np.array(counts)


def gaussian(rng, shape, scale, reach, cuts=(), held_as=jnp.bfloat16):
    gain = block_levels(rng, shape, cuts, -0.22, 0.18) if cuts else 1.0
    array = jax.random.normal(rng, shape, jnp.float32) * scale * gain
    return jnp.minimum(jnp.maximum(array, -reach), reach).astype(held_as)


def noise_with(own_key, shape, spread, most, cuts, heavy, kind=jnp.bfloat16):
    drawn = spread * jax.random.normal(own_key, shape, jnp.float32)
    if cuts:
        drawn = drawn * block_levels(own_key, shape, cuts, -0.22, 0.18)
    return jnp.clip(with_spikes(drawn, jax.random.fold_in(own_key, 3), *heavy), -most, most).astype(kind)


def setup_inputs(seed: int = 0) -> dict:
    streams_of = jax.random.split(jax.random.key(seed), 7)
    perturb = noise_with(streams_of[0], (MEMBERS, FIELDS, LEVELS, LAT, NLON), 1.0, 6.0, ((0, 16), (4, 16)), (0, 3, 16, 2.0))
    coef_x = jnp.clip(0.25 + 0.25 * jax.random.uniform(streams_of[1], (LEVELS, LAT, NLON), jnp.float32) ** block_levels(streams_of[1], (LEVELS, LAT, NLON), ((2, 16),), -0.2, 0.2), 0.25, 0.5)
    coef_y = jnp.clip(0.25 + 0.25 * jax.random.uniform(streams_of[2], (LEVELS, LAT, NLON), jnp.float32) ** block_levels(streams_of[2], (LEVELS, LAT, NLON), ((2, 16),), -0.2, 0.2), 0.25, 0.5)
    obs_values = gaussian(streams_of[3], (OBS_TOTAL,), 3.0, 12.0, ((0, 256),), jnp.float32)
    obs_tile_keys = jax.random.split(jax.random.fold_in(streams_of[4], 1), OBS_TOTAL // OBS_DEV)
    obs_tile_turns = jax.random.permutation(jax.random.fold_in(streams_of[4], 3), OBS_TOTAL // OBS_DEV)
    obs_tile = jax.vmap(lambda own, number: shared_out(jax.random.fold_in(streams_of[4], 2), own, number, OBS_DEV, TILES, 1, CAP, 2))(obs_tile_keys, obs_tile_turns).reshape((OBS_TOTAL, 1))
    obs_cell = plant(jax.random.randint(streams_of[5], (OBS_TOTAL,), 0, FIELDS * LEVELS * LAT * LON_DEV), jax.random.fold_in(streams_of[5], 1), 0, (FIELDS * LEVELS * LAT * LON_DEV) - 1).astype(jnp.int32)
    return {"perturb": perturb, "coef_x": coef_x, "coef_y": coef_y, "obs_values": obs_values, "obs_tile": obs_tile, "obs_cell": obs_cell}


def sweep_east(field, coef):
    flux = coef * (jnp.roll(field, -1, axis=-1) - field)
    return field + flux - jnp.roll(flux, 1, axis=-1)


def sweep_north(field, coef):
    flux = coef[..., :-1, :] * (field[..., 1:, :] - field[..., :-1, :])
    zero_row = jnp.zeros(field.shape[:-2] + (1, field.shape[-1]), jnp.float32)
    upper = jnp.concatenate([flux, zero_row], axis=-2)
    lower = jnp.concatenate([zero_row, flux], axis=-2)
    return field + upper - lower


def reference(perturb, coef_x, coef_y, obs_values, obs_tile, obs_cell):
    span = LAT * LON_DEV
    channel = obs_cell // span
    remain = obs_cell % span
    row = remain // LON_DEV
    column = obs_tile[:, 0] * LON_DEV + remain % LON_DEV
    flat = channel * (LAT * NLON) + row * NLON + column
    adjoint_field = jnp.zeros((FIELDS * LEVELS * LAT * NLON,), jnp.float32).at[flat].add(obs_values)
    adjoint_field = adjoint_field.reshape(FIELDS, LEVELS, LAT, NLON)

    def accumulate(total, member):
        widened = member.astype(jnp.float32)
        product = jnp.sum(widened * adjoint_field, axis=0)
        for step in range(SWEEPS):
            product = sweep_east(product, coef_x)
        for step in range(SWEEPS):
            product = sweep_north(product, coef_y)
        return total + widened * product[None], None

    start = jnp.zeros((FIELDS, LEVELS, LAT, NLON), jnp.float32)
    total, unused = lax.scan(accumulate, start, perturb)
    result = total / (MEMBERS - 1)
    return jnp.transpose(result, (2, 0, 1, 3))
```

```python
import functools

import jax
import jax.numpy as jnp
from jax import lax
from jax.experimental import pallas as pl
from jax.experimental.pallas import tpu as pltpu
from jax.sharding import PartitionSpec as P

FIELDS = 2
LEVELS = 2
SWEEPS = 6
LAT = 256
LON = 128
CAP = 384
LANES = 128
GROUPS = LAT // 8
BLOCKS = FIELDS * LEVELS * GROUPS
F32 = jnp.float32
BF16 = jnp.bfloat16
I32 = jnp.int32
NT = (((1,), (1,)), ((), ()))
NN = (((1,), (0,)), ((), ()))


def iota(shape, dim):
    return lax.broadcasted_iota(I32, shape, dim)


def dot(a, b, dims):
    return lax.dot_general(a, b, dims, preferred_element_type=F32)


def split(x):
    high = x.astype(BF16).astype(F32)
    return high, x - high


def pack_edges(load):
    lane = iota((8, LANES), 1)
    packed = jnp.zeros((8, LANES), F32)
    for g in range(8):
        place = (lane >= 16 * g) & (lane < 16 * g + 2 * SWEEPS)
        packed = jnp.where(place, pltpu.roll(load(g), SWEEPS + 16 * g, 1), packed)
    return packed


def merge_edges(west, east):
    return jnp.where(iota((8, LANES), 1) % 16 < SWEEPS, west, east)


def unpack_edges(merged, store):
    lane = iota((8, LANES), 1)
    halo = (lane < SWEEPS) | (lane >= LANES - SWEEPS)
    for g in range(8):
        store(g, jnp.where(halo, pltpu.roll(merged, LANES - SWEEPS - 16 * g, 1), 0.0))


def kernel(
    perturb_hbm, coef_x_hbm, coef_y_hbm, values_ref, tile_ref, cell_ref, out_ref,
    perturb_raw, coef_x_raw, coef_y_raw, perturb, perturb_halo, coef_x, coef_x_halo, coef_y,
    lists_out, lists_in, columns, total, partial, partial_in, adjoint, adjoint_halo,
    edges_out, edges_in, own_edges, near_edges, all_edges, product, terms, terms_in,
    load_sem, list_send, list_recv, edge_send, edge_recv, part_send, part_recv,
    adj_send, adj_recv, own_send, own_recv, all_send, all_recv, term_send, term_recv,
    *, mems, tiles, members,
):
    me_m, me_t = lax.axis_index("mem"), lax.axis_index("tile")
    west, east = lax.rem(me_t + tiles - 1, tiles), lax.rem(me_t + 1, tiles)
    blocks = values_ref.shape[0]
    slice_vecs = BLOCKS // mems

    def remote(src, dst, send, recv, m, t):
        return pltpu.make_async_remote_copy(
            src_ref=src, dst_ref=dst, send_sem=send, recv_sem=recv,
            device_id={"mem": m, "tile": t}, device_id_type=pl.DeviceIdType.MESH,
        )

    def other_m(d):
        return lax.rem(me_m + d, mems)

    def other_t(d):
        return lax.rem(me_t + d, tiles)

    loads = [
        pltpu.make_async_copy(src, dst, load_sem.at[i])
        for i, (src, dst) in enumerate(
            ((perturb_hbm, perturb_raw), (coef_x_hbm, coef_x_raw), (coef_y_hbm, coef_y_raw))
        )
    ]
    for copy in loads:
        copy.start()

    barrier = pltpu.get_barrier_semaphore()

    @pl.loop(1, mems)
    def _(d):
        pl.semaphore_signal(barrier, 1, device_id={"mem": other_m(d), "tile": me_t}, device_id_type=pl.DeviceIdType.MESH)

    @pl.loop(1, tiles)
    def _(d):
        pl.semaphore_signal(barrier, 1, device_id={"mem": me_m, "tile": other_t(d)}, device_id_type=pl.DeviceIdType.MESH)

    with jax.named_scope("bucket"):
        tile = tile_ref[...]
        hot = jnp.concatenate([jnp.where(tile == t, 1.0, 0.0) for t in range(tiles)], axis=0)
        hot16 = hot.astype(BF16)
        lane_r, lane_c = iota((LANES, 2 * LANES), 0), iota((LANES, 2 * LANES), 1)
        earlier = jnp.where((lane_r < lane_c) | (lane_c >= LANES), 1.0, 0.0).astype(BF16)
        counts = dot(hot16, earlier, NN)
        rows = tiles * blocks
        row, col = iota((rows, rows), 0), iota((rows, rows), 1)
        before = (row // blocks == col // blocks) & (col < row)
        base = dot(jnp.where(before, 1.0, 0.0).astype(BF16), counts[:, LANES:].astype(BF16), NN)
        ranks = hot * (counts[:, :LANES] + base)
        rank = ranks[0:blocks]
        for t in range(1, tiles):
            rank = rank + ranks[t * blocks : (t + 1) * blocks]
        rank = rank.astype(I32)
        slot_row, slot_lane = tile * 8 + (rank >> 7), rank & 127
        cell = cell_ref[...]
        value_parts = split(values_ref[...])
        cell_parts = [(cell & mask).astype(F32) for mask in (0x7F, 0x7F << 7, 0x7 << 14)]
        sums = None
        for start in range(0, blocks, 4):
            left, right = [], []
            for b in range(start, start + 4):
                at = iota((8 * tiles, LANES), 0)
                here = at == slot_row[b : b + 1]
                there = at == slot_row[b : b + 1] + 3
                left.append(
                    jnp.concatenate(
                        [jnp.where(here, part[b : b + 1], 0.0) for part in value_parts]
                        + [jnp.where(there, part[b : b + 1], 0.0) for part in cell_parts],
                        axis=0,
                    ).astype(BF16)
                )
                right.append(jnp.where(iota((LANES, LANES), 0) == slot_lane[b : b + 1], 1.0, 0.0).astype(BF16))
            got = dot(jnp.concatenate(left, axis=1), jnp.concatenate(right, axis=1), NT)
            sums = got if sums is None else sums + got
        packed = sums[0 : 8 * tiles]
        for i in range(1, 5):
            packed = packed + sums[8 * tiles * i : 8 * tiles * (i + 1)]
        lists_out[...] = packed.reshape(tiles, 8, LANES)

    pl.semaphore_wait(barrier, mems + tiles - 2)

    def list_copy(d):
        t = other_t(d)
        return remote(lists_out.at[t], lists_in.at[me_t], list_send.at[d], list_recv.at[d], me_m, t)

    @pl.loop(1, tiles)
    def _(d):
        list_copy(d).start()

    lists_in[me_t] = lists_out[me_t]

    with jax.named_scope("prepare"):
        for copy in loads:
            copy.wait()
        to, source = iota((LAT, LAT), 0), iota((LAT, LAT), 1)
        order = jnp.where(source == (to % 8) * GROUPS + to // 8, 1.0, 0.0).astype(BF16)

        @pl.loop(0, members * FIELDS * LEVELS)
        def _(i):
            perturb[i] = dot(order, perturb_raw[i], NN).reshape(GROUPS, 8, LANES)

        for l in range(LEVELS):
            for b in range(GROUPS):
                coef_x[l, b] = coef_x_raw[l, pl.ds(b, 8, stride=GROUPS), :]
                face = coef_y_raw[l, pl.ds(b, 8, stride=GROUPS), :]
                if b == GROUPS - 1:
                    face = jnp.where(iota((8, LANES), 0) < 7, face, 0.0)
                coef_y[l, b] = face

        chunks = GROUPS // 8

        @pl.loop(0, members * FIELDS * LEVELS)
        def _(i):
            for c in range(chunks):
                edges_out[i * chunks + c] = pack_edges(lambda g: perturb[i, c * 8 + g])

        for l in range(LEVELS):
            for c in range(chunks):
                edges_out[(members * FIELDS * LEVELS + l) * chunks + c] = pack_edges(lambda g: coef_x[l, c * 8 + g])

    @pl.loop(1, tiles)
    def _(d):
        list_copy(d).wait_recv()

    edge_copies = [
        remote(edges_out, edges_in.at[1], edge_send.at[0], edge_recv.at[1], me_m, west),
        remote(edges_out, edges_in.at[0], edge_send.at[1], edge_recv.at[0], me_m, east),
    ]
    for copy in edge_copies:
        copy.start()

    def part_copy(m):
        return remote(partial.at[m], partial_in.at[me_m], part_send.at[m], part_recv.at[me_m], m, me_t)

    with jax.named_scope("deposit"):
        lists = lists_in[...]
        cells = lists.astype(I32)
        grid_row, grid_col = cells >> 7, cells & 127
        grid_row = (grid_row & ~255) | ((grid_row & 31) << 3) | ((grid_row >> 5) & 7)
        high, low = split(lists)
        per_list = CAP // LANES
        for t in range(tiles):
            for j in range(per_list):
                k = (t * per_list + j) * LANES
                here = iota((LANES, LANES), 0) == grid_col[t, 3 + j : 4 + j]
                columns[0:LANES, k : k + LANES] = jnp.where(here, high[t, j : j + 1], 0.0).astype(BF16)
                columns[LANES : 2 * LANES, k : k + LANES] = jnp.where(here, low[t, j : j + 1], 0.0).astype(BF16)

        @pl.loop(0, 4)
        def _(i):
            quarter = lax.rem(me_m // (mems // 4) + i, 4)
            at = iota((256, LANES), 0) + quarter * 256
            for t in range(0, tiles, 2):
                left = jnp.concatenate(
                    [
                        jnp.where(at == grid_row[u, 3 + j : 4 + j], 1.0, 0.0).astype(BF16)
                        for u in (t, t + 1)
                        for j in range(per_list)
                    ],
                    axis=1,
                )
                got = dot(left, columns[:, t * CAP : (t + 2) * CAP], NT)
                total[...] = got if t == 0 else total[...] + got
            whole = total[:, :LANES] + total[:, LANES:]
            for part in range(mems // 4):
                m = quarter * (mems // 4) + part
                rows = 8 * slice_vecs
                piece = whole[part * rows : (part + 1) * rows].reshape(slice_vecs, 8, LANES)
                partial[m] = piece

                @pl.when(m != me_m)
                def _():
                    part_copy(m).start()

    with jax.named_scope("halos"):
        for copy in edge_copies:
            copy.wait_recv()

        @pl.loop(0, members * FIELDS * LEVELS)
        def _(i):
            for c in range(chunks):
                merged = merge_edges(edges_in[0, i * chunks + c], edges_in[1, i * chunks + c])

                def store(g, x):
                    perturb_halo[i, c * 8 + g] = x

                unpack_edges(merged, store)

        for l in range(LEVELS):
            for c in range(chunks):
                at_edge = (members * FIELDS * LEVELS + l) * chunks + c

                def store(g, x):
                    coef_x_halo[l, c * 8 + g] = x

                unpack_edges(merge_edges(edges_in[0, at_edge], edges_in[1, at_edge]), store)

    def from_m(dst, send, recv, m):
        return remote(dst.at[m], dst.at[m], send.at[m], recv.at[m], m, me_t)

    with jax.named_scope("field_sum"):
        field = partial[me_m]

        def add(d, acc):
            m = other_m(d)
            from_m(partial_in, part_send, part_recv, m).wait_recv()
            return acc + partial_in[m]

        field = lax.fori_loop(1, mems, add, field)
        adjoint[me_m] = field

    def adj_copy(d):
        return remote(adjoint.at[me_m], adjoint.at[me_m], adj_send.at[d], adj_recv.at[me_m], other_m(d), me_t)

    def all_copy(d):
        return remote(all_edges.at[me_m], all_edges.at[me_m], all_send.at[d], all_recv.at[me_m], other_m(d), me_t)

    packs = slice_vecs // 8
    for c in range(packs):
        own_edges[c] = pack_edges(lambda g: field[c * 8 + g])
    own_copies = [
        remote(own_edges, near_edges.at[1], own_send.at[0], own_recv.at[1], me_m, west),
        remote(own_edges, near_edges.at[0], own_send.at[1], own_recv.at[0], me_m, east),
    ]
    for copy in own_copies:
        copy.start()

    @pl.loop(1, mems)
    def _(d):
        adj_copy(d).start()

    for copy in own_copies:
        copy.wait_recv()
    for c in range(packs):
        all_edges[me_m, c] = merge_edges(near_edges[0, c], near_edges[1, c])

    @pl.loop(1, mems)
    def _(d):
        all_copy(d).start()

    @pl.loop(1, mems)
    def _(d):
        m = other_m(d)
        from_m(adjoint, adj_send, adj_recv, m).wait_recv()
        from_m(all_edges, all_send, all_recv, m).wait_recv()

    with jax.named_scope("adjoint_halo"):

        @pl.loop(0, BLOCKS // 8)
        def _(i):
            def store(g, x):
                adjoint_halo[i // packs, (i % packs) * 8 + g] = x

            unpack_edges(all_edges[i // packs, i % packs], store)

    first_lane, last_lane = iota((8, LANES), 1) == 0, iota((8, LANES), 1) == LANES - 1

    def east_steps(l):
        @pl.loop(0, GROUPS)
        def _(b):
            adj, adj_h = [], []
            for f in range(FIELDS):
                vector = (f * LEVELS + l) * GROUPS + b
                adj.append(adjoint[vector // slice_vecs, vector % slice_vecs])
                adj_h.append(adjoint_halo[vector // slice_vecs, vector % slice_vecs])
            c, ch = coef_x[l, b], coef_x_halo[l, b]
            for k in range(members):
                v = vh = 0.0
                for f in range(FIELDS):
                    i = (k * FIELDS + f) * LEVELS + l
                    v = v + perturb[i, b] * adj[f]
                    vh = vh + perturb_halo[i, b] * adj_h[f]
                for _ in range(SWEEPS):
                    near, near_h = pltpu.roll(v, LANES - 1, 1), pltpu.roll(vh, LANES - 1, 1)
                    flux = c * (jnp.where(last_lane, near_h, near) - v)
                    flux_h = ch * (jnp.where(last_lane, near, near_h) - vh)
                    back, back_h = pltpu.roll(flux, 1, 1), pltpu.roll(flux_h, 1, 1)
                    v = v + flux - jnp.where(first_lane, back_h, back)
                    vh = vh + flux_h - jnp.where(first_lane, back, back_h)
                product[l * members + k, b] = v

    def north_steps(l):
        @pl.loop(0, members)
        def _(k):
            v = [product[l * members + k, b] for b in range(GROUPS)]
            for _ in range(SWEEPS):
                flux = [
                    coef_y[l, b] * ((v[b + 1] if b + 1 < GROUPS else pltpu.roll(v[0], 7, 0)) - v[b])
                    for b in range(GROUPS)
                ]
                v = [
                    v[b] + flux[b] - (flux[b - 1] if b else pltpu.roll(flux[GROUPS - 1], 1, 0))
                    for b in range(GROUPS)
                ]
            for b in range(GROUPS):
                product[l * members + k, b] = v[b]

    def increments(l):
        @pl.loop(0, GROUPS)
        def _(b):
            weights = [product[l * members + k, b] for k in range(members)]
            for f in range(FIELDS):
                acc = weights[0] * perturb[f * LEVELS + l, b]
                for k in range(1, members):
                    acc = acc + weights[k] * perturb[(k * FIELDS + f) * LEVELS + l, b]
                terms[l, pl.ds(2 * b + f, 8, stride=2 * GROUPS), :] = acc

    term_rows = 2 * LAT // mems

    def term_slice(ref, l, m):
        return ref.at[l, pl.ds(pl.multiple_of(m * term_rows, term_rows), term_rows)]

    def term_copy(l, d):
        m = other_m(d)
        return remote(
            term_slice(terms, l, m), term_slice(terms_in, l, me_m),
            term_send.at[l, d], term_recv.at[l, d], m, me_t,
        )

    for l in range(LEVELS):
        with jax.named_scope("east"):
            east_steps(l)
        with jax.named_scope("north"):
            north_steps(l)
        with jax.named_scope("increments"):
            increments(l)

        @pl.loop(1, mems)
        def _(d):
            term_copy(l, d).start()

    with jax.named_scope("increment_sum"):
        for l in range(LEVELS):
            mine = pl.ds(pl.multiple_of(me_m * term_rows, term_rows), term_rows)
            acc = terms[l, mine]

            def add(d, acc):
                term_copy(l, d).wait_recv()
                m = lax.rem(me_m + mems - d, mems)
                return acc + terms_in[l, pl.ds(pl.multiple_of(m * term_rows, term_rows), term_rows)]

            acc = lax.fori_loop(1, mems, add, acc)
            out_ref[l] = acc * (1.0 / (members * mems - 1))

    for copy in edge_copies + own_copies:
        copy.wait_send()

    @pl.loop(1, tiles)
    def _(d):
        list_copy(d).wait_send()

    @pl.loop(1, mems)
    def _(d):
        part_copy(other_m(d)).wait_send()
        adj_copy(d).wait_send()
        all_copy(d).wait_send()
        for l in range(LEVELS):
            term_copy(l, d).wait_send()


def on_device(perturb, coef_x, coef_y, obs_values, obs_tile, obs_cell):
    mems, tiles = lax.axis_size("mem"), lax.axis_size("tile")
    members = perturb.shape[0]
    channels = members * FIELDS * LEVELS
    slice_vecs = BLOCKS // mems
    edge_vecs = (channels + LEVELS) * GROUPS // 8
    term_rows = 2 * LAT // mems
    dma = pltpu.SemaphoreType.DMA

    def vectors(*shape):
        return pltpu.VMEM((*shape, 8, LANES), F32)

    out = pl.pallas_call(
        functools.partial(kernel, mems=mems, tiles=tiles, members=members),
        out_shape=jax.ShapeDtypeStruct((LEVELS, term_rows, LANES), F32),
        in_specs=[pl.BlockSpec(memory_space=pl.ANY)] * 3 + [pl.BlockSpec(memory_space=pltpu.VMEM)] * 3,
        out_specs=pl.BlockSpec(memory_space=pltpu.VMEM),
        scratch_shapes=[
            pltpu.VMEM((channels, LAT, LON), BF16),
            pltpu.VMEM((LEVELS, LAT, LON), F32),
            pltpu.VMEM((LEVELS, LAT, LON), F32),
            vectors(channels, GROUPS),
            vectors(channels, GROUPS),
            vectors(LEVELS, GROUPS),
            vectors(LEVELS, GROUPS),
            vectors(LEVELS, GROUPS),
            vectors(tiles),
            vectors(tiles),
            pltpu.VMEM((2 * LANES, tiles * CAP), BF16),
            pltpu.VMEM((256, 2 * LANES), F32),
            vectors(mems, slice_vecs),
            vectors(mems, slice_vecs),
            vectors(mems, slice_vecs),
            vectors(mems, slice_vecs),
            vectors(edge_vecs),
            vectors(2, edge_vecs),
            vectors(slice_vecs // 8),
            vectors(2, slice_vecs // 8),
            vectors(mems, slice_vecs // 8),
            vectors(LEVELS * members, GROUPS),
            pltpu.VMEM((LEVELS, 2 * LAT, LANES), F32),
            pltpu.VMEM((LEVELS, 2 * LAT, LANES), F32),
            dma((3,)),
            dma((tiles,)), dma((tiles,)),
            dma((2,)), dma((2,)),
            dma((mems,)), dma((mems,)),
            dma((mems,)), dma((mems,)),
            dma((2,)), dma((2,)),
            dma((mems,)), dma((mems,)),
            dma((LEVELS, mems)), dma((LEVELS, mems)),
        ],
        compiler_params=pltpu.CompilerParams(
            collective_id=0, has_side_effects=True, vmem_limit_bytes=56 * 2**20
        ),
    )(
        perturb.reshape(channels, LAT, LON),
        coef_x,
        coef_y,
        obs_values.reshape(-1, LANES),
        obs_tile.reshape(-1, LANES),
        obs_cell.reshape(-1, LANES),
    )
    out = out.reshape(LEVELS, LAT // mems, FIELDS, LANES)
    return jnp.transpose(out, (1, 2, 0, 3))


def solution(mesh):
    return jax.shard_map(
        on_device,
        mesh=mesh,
        in_specs=(
            P("mem", None, None, None, "tile"),
            P(None, None, "tile"),
            P(None, None, "tile"),
            P(("mem", "tile")),
            P(("mem", "tile"), None),
            P(("mem", "tile")),
        ),
        out_specs=P("mem", None, None, "tile"),
        check_vma=False,
    )
```

```python
import functools

import jax
import jax.numpy as jnp
from jax import lax
from jax.experimental import pallas as pl
from jax.experimental.pallas import tpu as pltpu
from jax.sharding import PartitionSpec as P

FIELDS = 2
LEVELS = 2
SWEEPS = 6
LAT = 256
LON = 128
CAP = 384
LANES = 128
GROUPS = LAT // 8
HALO = 8
WIDE = LON + 2 * HALO
STEPS = WIDE // 8
HALVES = LAT // LANES
CHIPS = 8
PART = LON // 4
F32 = jnp.float32
BF16 = jnp.bfloat16
I32 = jnp.int32
NT = (((1,), (1,)), ((), ()))
NN = (((1,), (0,)), ((), ()))


def iota(shape, dim):
    return lax.broadcasted_iota(I32, shape, dim)


def dot(a, b, dims):
    return lax.dot_general(a, b, dims, preferred_element_type=F32)


def split(x):
    high = x.astype(BF16).astype(F32)
    return high, x - high


def kernel(
    perturb_hbm, coef_x_hbm, coef_y_hbm, values_ref, tile_ref, cell_ref, out_ref,
    perturb_raw, coef_x_raw, coef_y_raw, perturb, perturb_t, perturb_g, coef_t, coef_g, coef_y,
    lists_out, lists_in, columns, total, partial, sibling_in, partial_in, adjoint_t, adjoint_g,
    diffused, product, terms, terms_sibling, terms_in,
    load_sem, list_send, list_recv, edge_send, edge_recv, half_send, half_recv, part_send, part_recv,
    adj_send, adj_recv, pass_send, pass_recv, halo_send, halo_recv, halo_pass_send, halo_pass_recv,
    near_send, near_recv, term_send, term_recv,
    *, tiles, members,
):
    me_m, me_t = lax.axis_index("mem"), lax.axis_index("tile")
    chip, core = me_m // 2, lax.rem(me_m, 2)
    sibling = 2 * chip + 1 - core
    west, east = lax.rem(me_t + tiles - 1, tiles), lax.rem(me_t + 1, tiles)
    blocks = values_ref.shape[0]
    channels = members * FIELDS * LEVELS

    def remote(src, dst, send, recv, m, t):
        return pltpu.make_async_remote_copy(
            src_ref=src, dst_ref=dst, send_sem=send, recv_sem=recv,
            device_id={"mem": m, "tile": t}, device_id_type=pl.DeviceIdType.MESH,
        )

    def signal(m, t):
        pl.semaphore_signal(
            barrier, 1, device_id={"mem": m, "tile": t}, device_id_type=pl.DeviceIdType.MESH
        )

    def other_chip(d):
        return lax.rem(chip + d, CHIPS)

    def other_t(d):
        return lax.rem(me_t + d, tiles)

    loads = [
        pltpu.make_async_copy(src, dst, load_sem.at[i])
        for i, (src, dst) in enumerate(
            ((perturb_hbm, perturb_raw), (coef_x_hbm, coef_x_raw), (coef_y_hbm, coef_y_raw))
        )
    ]
    for copy in loads:
        copy.start()

    barrier = pltpu.get_barrier_semaphore()
    signal(sibling, me_t)

    @pl.loop(1, CHIPS)
    def _(d):
        m = 2 * other_chip(d) + core
        signal(m, me_t)
        signal(m, west)
        signal(m, east)

    @pl.loop(1, tiles)
    def _(d):
        signal(me_m, other_t(d))

    with jax.named_scope("bucket"):
        tile = tile_ref[...]
        hot = jnp.concatenate([jnp.where(tile == t, 1.0, 0.0) for t in range(tiles)], axis=0)
        hot16 = hot.astype(BF16)
        lane_r, lane_c = iota((LANES, 2 * LANES), 0), iota((LANES, 2 * LANES), 1)
        earlier = jnp.where((lane_r < lane_c) | (lane_c >= LANES), 1.0, 0.0).astype(BF16)
        counts = dot(hot16, earlier, NN)
        rows = tiles * blocks
        row, col = iota((rows, rows), 0), iota((rows, rows), 1)
        before = (row // blocks == col // blocks) & (col < row)
        base = dot(jnp.where(before, 1.0, 0.0).astype(BF16), counts[:, LANES:].astype(BF16), NN)
        ranks = hot * (counts[:, :LANES] + base)
        rank = ranks[0:blocks]
        for t in range(1, tiles):
            rank = rank + ranks[t * blocks : (t + 1) * blocks]
        rank = rank.astype(I32)
        slot_row, slot_lane = tile * 8 + (rank >> 7), rank & 127
        cell = cell_ref[...]
        value_parts = split(values_ref[...])
        cell_parts = [(cell & mask).astype(F32) for mask in (0x7F, 0x7F << 7, 0x7 << 14)]
        sums = None
        for start in range(0, blocks, 4):
            left, right = [], []
            for b in range(start, start + 4):
                at = iota((8 * tiles, LANES), 0)
                here = at == slot_row[b : b + 1]
                there = at == slot_row[b : b + 1] + 3
                left.append(
                    jnp.concatenate(
                        [jnp.where(here, part[b : b + 1], 0.0) for part in value_parts]
                        + [jnp.where(there, part[b : b + 1], 0.0) for part in cell_parts],
                        axis=0,
                    ).astype(BF16)
                )
                right.append(jnp.where(iota((LANES, LANES), 0) == slot_lane[b : b + 1], 1.0, 0.0).astype(BF16))
            got = dot(jnp.concatenate(left, axis=1), jnp.concatenate(right, axis=1), NT)
            sums = got if sums is None else sums + got
        packed = sums[0 : 8 * tiles]
        for i in range(1, 5):
            packed = packed + sums[8 * tiles * i : 8 * tiles * (i + 1)]
        lists_out[...] = packed.reshape(tiles, 8, LANES)

    for copy in loads:
        copy.wait()
    with jax.named_scope("prepare"):
        to, source = iota((LAT, LAT), 0), iota((LAT, LAT), 1)
        order = jnp.where(source == (to % 8) * GROUPS + to // 8, 1.0, 0.0).astype(BF16)
        same = jnp.where(iota((LON, LON), 0) == iota((LON, LON), 1), 1.0, 0.0).astype(BF16)

        @pl.loop(0, channels)
        def _(i):
            rows = dot(order, perturb_raw[i], NN)
            perturb[i] = rows.reshape(GROUPS, 8, LANES)
            turned = dot(same, rows.astype(BF16), NT)
            for h in range(HALVES):
                perturb_t[i, h, HALO : HALO + LON] = turned[:, h * LANES : (h + 1) * LANES]

        for l in range(LEVELS):
            faces = []
            for b in range(GROUPS):
                faces.append(coef_x_raw[l, pl.ds(b, 8, stride=GROUPS), :])
                face = coef_y_raw[l, pl.ds(b, 8, stride=GROUPS), :]
                if b == GROUPS - 1:
                    face = jnp.where(iota((8, LANES), 0) < 7, face, 0.0)
                coef_y[l, b] = face
            faces = jnp.concatenate(faces, axis=0)
            for h in range(HALVES):
                coef_t[l, h, HALO : HALO + LON] = faces[h * LANES : (h + 1) * LANES].T

    pl.semaphore_wait(barrier, 1 + 3 * (CHIPS - 1) + tiles - 1)

    def list_copy(d):
        t = other_t(d)
        return remote(lists_out.at[t], lists_in.at[me_t], list_send.at[d], list_recv.at[d], me_m, t)

    @pl.loop(1, tiles)
    def _(d):
        list_copy(d).start()

    lists_in[me_t] = lists_out[me_t]

    def edge(ref, start):
        return ref.at[:, :, pl.ds(start, HALO)]

    edge_copies = []
    for i, ref in enumerate((perturb_t, coef_t)):
        edge_copies.append(
            remote(edge(ref, LON), edge(ref, 0), edge_send.at[i, 0], edge_recv.at[i, 0], me_m, east)
        )
        edge_copies.append(
            remote(edge(ref, HALO), edge(ref, HALO + LON), edge_send.at[i, 1], edge_recv.at[i, 1], me_m, west)
        )
    for copy in edge_copies:
        copy.start()

    @pl.loop(1, tiles)
    def _(d):
        list_copy(d).wait_recv()

    half_copy = remote(partial.at[1 - core], sibling_in, half_send.at[0], half_recv.at[0], sibling, me_t)

    with jax.named_scope("deposit"):
        lists = lists_in[...]
        cells = lists.astype(I32)
        grid_row = (cells >> 15) * LON + (cells & (LON - 1))
        grid_lane = (cells >> 7) & (LAT - 1)
        grid_lane = (grid_lane % GROUPS) * 8 + grid_lane // GROUPS
        high, low = split(lists)
        per_list = CAP // LANES
        for t in range(tiles):
            for j in range(per_list):
                k = (t * per_list + j) * LANES
                here = iota((LAT, LANES), 0) == grid_lane[t, 3 + j : 4 + j]
                columns[0:LAT, k : k + LANES] = jnp.where(here, high[t, j : j + 1], 0.0).astype(BF16)
                columns[LAT : 2 * LAT, k : k + LANES] = jnp.where(here, low[t, j : j + 1], 0.0).astype(BF16)
        span = 4
        for f in (1 - core, core):
            at = iota((2 * LON, LANES), 0) + f * (2 * LON)
            for t in range(0, tiles, span):
                left = jnp.concatenate(
                    [
                        jnp.where(at == grid_row[u, 3 + j : 4 + j], 1.0, 0.0).astype(BF16)
                        for u in range(t, t + span)
                        for j in range(per_list)
                    ],
                    axis=1,
                )
                got = dot(left, columns[:, t * CAP : (t + span) * CAP], NT)
                if t == 0:
                    total[...] = got
                elif t + span < tiles:
                    total[...] += got
            for h in range(HALVES):
                lanes = slice(h * LANES, (h + 1) * LANES)
                lows = slice(LAT + h * LANES, LAT + (h + 1) * LANES)
                partial[f, h] = (total[:, lanes] + got[:, lanes]) + (total[:, lows] + got[:, lows])
            if f is not core:
                half_copy.start()

    def rows(c):
        return pl.ds(pl.multiple_of(c * PART, PART), PART)

    def part_copy(d):
        c = other_chip(d)
        return remote(
            partial.at[core, :, rows(c)], partial_in.at[chip], part_send.at[d], part_recv.at[d], 2 * c + core, me_t
        )

    half_copy.wait_recv()
    with jax.named_scope("sibling_sum"):
        for h in range(HALVES):
            partial[core, h] += sibling_in[h]

    @pl.loop(1, CHIPS)
    def _(d):
        part_copy(d).start()

    for copy in edge_copies:
        copy.wait_recv()

    def gather(source, target, i):
        for h in range(HALVES):
            for b in range(STEPS):
                target[i, h, b] = source[i, h, pl.ds(b, 8, stride=STEPS), :]

    with jax.named_scope("gather"):

        @pl.loop(0, channels)
        def _(i):
            gather(perturb_t, perturb_g, i)

        for l in range(LEVELS):
            gather(coef_t, coef_g, l)

    def block(f, c):
        start = pl.multiple_of(HALO + lax.rem(c, 4) * PART, 8)
        return adjoint_t.at[f * LEVELS + c // 4, :, pl.ds(start, PART)]

    field = partial[core, :, rows(chip)]

    def add_part(d, acc):
        part_copy(d).wait_recv()
        return acc + partial_in[other_chip(CHIPS - d)]

    block(core, chip)[...] = lax.fori_loop(1, CHIPS, add_part, field)

    def adj_copy(d):
        mine = block(core, chip)
        return remote(mine, mine, adj_send.at[d], adj_recv.at[chip], 2 * other_chip(d) + core, me_t)

    def adj_from(c):
        there = block(core, c)
        return remote(there, there, adj_send.at[0], adj_recv.at[c], 2 * other_chip(1) + core, me_t)

    def pass_copy(c, f):
        there = block(f, c)
        return remote(there, there, pass_send.at[c], pass_recv.at[c], sibling, me_t)

    def halo_at(f, l, start):
        return adjoint_t.at[f * LEVELS + l, :, pl.ds(start, HALO)]

    def halo_copy(c, side):
        l = chip // 4
        source = halo_at(core, l, HALO if side else LON)
        target = halo_at(core, l, HALO + LON if side else 0)
        return remote(
            source, target, halo_send.at[c], halo_recv.at[l, side], 2 * c + core, west if side else east
        )

    def halo_from(l, side):
        target = halo_at(core, l, HALO + LON if side else 0)
        return remote(target, target, halo_send.at[0], halo_recv.at[l, side], me_m, east)

    def halo_pass(f, l, side):
        target = halo_at(f, l, HALO + LON if side else 0)
        return remote(target, target, halo_pass_send.at[l, side], halo_pass_recv.at[l, side], sibling, me_t)

    @pl.loop(1, CHIPS)
    def _(d):
        adj_copy(d).start()

    for side in (0, 1):

        @pl.when(lax.rem(chip, 4) == (0 if side else 3))
        def _():
            @pl.loop(0, CHIPS)
            def _(c):
                halo_copy(c, side).start()

    pass_copy(chip, core).start()

    @pl.loop(1, CHIPS)
    def _(d):
        c = other_chip(d)
        adj_from(c).wait_recv()
        pass_copy(c, core).start()

    for l in range(LEVELS):
        for side in (0, 1):
            halo_from(l, side).wait_recv()
            halo_pass(core, l, side).start()

    def east_steps(l):
        for h in range(HALVES):
            for f in range(FIELDS):
                for b in range(STEPS):
                    adjoint_g[f, h, b] = adjoint_t[f * LEVELS + l, h, pl.ds(b, 8, stride=STEPS), :]

        for h in range(HALVES):

            @pl.loop(0, members)
            def _(k):
                i = k * (FIELDS * LEVELS) + l
                v = [
                    perturb_g[i, h, b] * adjoint_g[0, h, b] + perturb_g[i + LEVELS, h, b] * adjoint_g[1, h, b]
                    for b in range(STEPS)
                ]
                for _ in range(SWEEPS):
                    following = v[1:] + [pltpu.roll(v[0], 7, 0)]
                    flux = [coef_g[l, h, b] * (following[b] - v[b]) for b in range(STEPS)]
                    before = [pltpu.roll(flux[-1], 1, 0)] + flux[:-1]
                    v = [v[b] + flux[b] - before[b] for b in range(STEPS)]
                for b in range(STEPS):
                    diffused[k, h, pl.ds(b, 8, stride=STEPS), :] = v[b]

    def turn(l):
        @pl.loop(0, members)
        def _(k):
            for h in range(HALVES):
                turned = diffused[k, h, HALO : HALO + LON].T
                half = GROUPS // HALVES
                product[l * members + k, h * half : (h + 1) * half] = turned.reshape(half, 8, LANES)

    def north_steps(l):
        @pl.loop(0, members)
        def _(k):
            v = [product[l * members + k, b] for b in range(GROUPS)]
            for _ in range(SWEEPS):
                following = v[1:] + [pltpu.roll(v[0], 7, 0)]
                flux = [coef_y[l, b] * (following[b] - v[b]) for b in range(GROUPS)]
                before = [pltpu.roll(flux[-1], 1, 0)] + flux[:-1]
                v = [v[b] + flux[b] - before[b] for b in range(GROUPS)]
            for b in range(GROUPS):
                product[l * members + k, b] = v[b]

    share = LAT // (2 * CHIPS)

    def increments(l, half):
        @pl.loop(0, share)
        def _(b):
            at = half * share + b
            weights = [product[l * members + k, at] for k in range(members)]
            for f in range(FIELDS):
                acc = weights[0] * perturb[f * LEVELS + l, at]
                for k in range(1, members):
                    acc = acc + weights[k] * perturb[(k * FIELDS + f) * LEVELS + l, at]
                terms[l, half, pl.ds(2 * b + f, 8, stride=2 * share), :] = acc

    def out_rows(c):
        return pl.ds(pl.multiple_of(c * 2 * share, 2 * share), 2 * share)

    def near_copy(l):
        return remote(terms.at[l, 1 - core], terms_sibling.at[l], near_send.at[l], near_recv.at[l], sibling, me_t)

    def term_copy(l, d):
        c = other_chip(d)
        return remote(
            terms.at[l, core, out_rows(c)], terms_in.at[l, chip],
            term_send.at[l, d], term_recv.at[l, d], 2 * c + core, me_t,
        )

    def send_terms(l):
        near_copy(l).wait_recv()
        terms[l, core] += terms_sibling[l]

        @pl.loop(1, CHIPS)
        def _(d):
            term_copy(l, d).start()

    for l in range(LEVELS):
        for c in range(4 * l, 4 * l + 4):
            pass_copy(c, 1 - core).wait_recv()
        for side in (0, 1):
            halo_pass(1 - core, l, side).wait_recv()
        with jax.named_scope("east"):
            east_steps(l)
        with jax.named_scope("turn"):
            turn(l)
        if l:
            send_terms(l - 1)
        with jax.named_scope("north"):
            north_steps(l)
        with jax.named_scope("increments"):
            increments(l, 1 - core)
        near_copy(l).start()
        with jax.named_scope("increments"):
            increments(l, core)
    send_terms(LEVELS - 1)

    for l in range(LEVELS):

        def add_term(d, acc):
            term_copy(l, d).wait_recv()
            return acc + terms_in[l, other_chip(CHIPS - d)]

        acc = lax.fori_loop(1, CHIPS, add_term, terms[l, core, out_rows(chip)])
        out_ref[l] = acc * (1.0 / (2 * CHIPS * members - 1))

    for copy in edge_copies + [half_copy]:
        copy.wait_send()

    @pl.loop(1, tiles)
    def _(d):
        list_copy(d).wait_send()

    @pl.loop(1, CHIPS)
    def _(d):
        part_copy(d).wait_send()
        adj_copy(d).wait_send()
        for l in range(LEVELS):
            term_copy(l, d).wait_send()

    @pl.loop(0, CHIPS)
    def _(c):
        pass_copy(c, core).wait_send()

    for side in (0, 1):

        @pl.when(lax.rem(chip, 4) == (0 if side else 3))
        def _():
            @pl.loop(0, CHIPS)
            def _(c):
                halo_copy(c, side).wait_send()

    for l in range(LEVELS):
        near_copy(l).wait_send()
        for side in (0, 1):
            halo_pass(core, l, side).wait_send()


def on_device(perturb, coef_x, coef_y, obs_values, obs_tile, obs_cell):
    tiles = lax.axis_size("tile")
    members = perturb.shape[0]
    channels = members * FIELDS * LEVELS
    share = LAT // (2 * CHIPS)
    dma = pltpu.SemaphoreType.DMA

    def rows(*shape):
        return pltpu.VMEM((*shape, LANES), F32)

    out = pl.pallas_call(
        functools.partial(kernel, tiles=tiles, members=members),
        out_shape=jax.ShapeDtypeStruct((LEVELS, 2 * share, LANES), F32),
        in_specs=[pl.BlockSpec(memory_space=pl.ANY)] * 3 + [pl.BlockSpec(memory_space=pltpu.VMEM)] * 3,
        out_specs=pl.BlockSpec(memory_space=pltpu.VMEM),
        scratch_shapes=[
            pltpu.VMEM((channels, LAT, LON), BF16),
            rows(LEVELS, LAT),
            rows(LEVELS, LAT),
            rows(channels, GROUPS, 8),
            rows(channels, HALVES, WIDE),
            rows(channels, HALVES, STEPS, 8),
            rows(LEVELS, HALVES, WIDE),
            rows(LEVELS, HALVES, STEPS, 8),
            rows(LEVELS, GROUPS, 8),
            rows(tiles, 8),
            rows(tiles, 8),
            pltpu.VMEM((2 * LAT, tiles * CAP), BF16),
            pltpu.VMEM((LEVELS * LON, 2 * LAT), F32),
            rows(FIELDS, HALVES, LEVELS * LON),
            rows(HALVES, LEVELS * LON),
            rows(CHIPS, HALVES, PART),
            rows(FIELDS * LEVELS, HALVES, WIDE),
            rows(FIELDS, HALVES, STEPS, 8),
            rows(members, HALVES, WIDE),
            rows(LEVELS * members, GROUPS, 8),
            rows(LEVELS, 2, LAT),
            rows(LEVELS, LAT),
            rows(LEVELS, CHIPS, 2 * share),
            dma((3,)),
            dma((tiles,)), dma((tiles,)),
            dma((2, 2)), dma((2, 2)),
            dma((1,)), dma((1,)),
            dma((CHIPS,)), dma((CHIPS,)),
            dma((CHIPS,)), dma((CHIPS,)),
            dma((CHIPS,)), dma((CHIPS,)),
            dma((CHIPS,)), dma((LEVELS, 2)),
            dma((LEVELS, 2)), dma((LEVELS, 2)),
            dma((LEVELS,)), dma((LEVELS,)),
            dma((LEVELS, CHIPS)), dma((LEVELS, CHIPS)),
        ],
        compiler_params=pltpu.CompilerParams(
            collective_id=0, has_side_effects=True, vmem_limit_bytes=56 * 2**20
        ),
    )(
        perturb.reshape(channels, LAT, LON),
        coef_x,
        coef_y,
        obs_values.reshape(-1, LANES),
        obs_tile.reshape(-1, LANES),
        obs_cell.reshape(-1, LANES),
    )
    out = out.reshape(LEVELS, share, FIELDS, LANES)
    return jnp.transpose(out, (1, 2, 0, 3))


def solution(mesh):
    return jax.shard_map(
        on_device,
        mesh=mesh,
        in_specs=(
            P("mem", None, None, None, "tile"),
            P(None, None, "tile"),
            P(None, None, "tile"),
            P(("mem", "tile")),
            P(("mem", "tile"), None),
            P(("mem", "tile")),
        ),
        out_specs=P("mem", None, None, "tile"),
        check_vma=False,
    )
```

```python
import functools

import jax
import jax.numpy as jnp
from jax import lax
from jax.experimental import pallas as pl
from jax.experimental.pallas import tpu as pltpu
from jax.sharding import PartitionSpec as P

FIELDS = 2
LEVELS = 2
SWEEPS = 6
LAT = 256
LON = 128
CAP = 384
LANES = 128
GROUPS = LAT // 8
HALO = 8
WIDE = LON + 2 * HALO
STEPS = WIDE // 8
HALVES = LAT // LANES
CHIPS = 8
DEPTH = 8
OFFSETS = ((0, 0), (0, 1), (0, 7), (0, 2), (0, 6), (1, 0), (0, 3), (0, 5), (1, 1), (1, 7), (0, 4), (1, 2), (1, 6), (1, 3), (1, 5), (1, 4))
PART = LON // 4
F32 = jnp.float32
BF16 = jnp.bfloat16
I32 = jnp.int32
NT = (((1,), (1,)), ((), ()))
NN = (((1,), (0,)), ((), ()))


def iota(shape, dim):
    return lax.broadcasted_iota(I32, shape, dim)


def dot(a, b, dims):
    return lax.dot_general(a, b, dims, preferred_element_type=F32)


def split(x):
    high = x.astype(BF16).astype(F32)
    return high, x - high


def kernel(
    perturb_hbm, coef_x_hbm, coef_y_hbm, values_ref, tile_ref, cell_ref, out_ref,
    perturb_raw, coef_x_raw, coef_y_raw, perturb, perturb_out, perturb_t, perturb_g, coef_t, coef_g, coef_y,
    lists_out, lists_in, total, partial, partial_in, adjoint_t, adjoint_g, diffused, product, terms, terms_in,
    load_sem, list_send, list_recv, share_send, share_recv, edge_send, edge_recv, part_send, part_recv,
    adj_send, adj_recv, halo_send, halo_recv, term_send, term_recv,
    *, tiles, members,
):
    me_m, me_t = lax.axis_index("mem"), lax.axis_index("tile")
    chip, core = me_m // 2, lax.rem(me_m, 2)
    sibling = 2 * chip + 1 - core
    west, east = lax.rem(me_t + tiles - 1, tiles), lax.rem(me_t + 1, tiles)
    blocks = values_ref.shape[0]
    mems = 2 * CHIPS
    own = members * FIELDS

    def remote(src, dst, send, recv, m, t):
        return pltpu.make_async_remote_copy(
            src_ref=src, dst_ref=dst, send_sem=send, recv_sem=recv,
            device_id={"mem": m, "tile": t}, device_id_type=pl.DeviceIdType.MESH,
        )

    def signal(m, t):
        pl.semaphore_signal(
            barrier, 1, device_id={"mem": m, "tile": t}, device_id_type=pl.DeviceIdType.MESH
        )

    def other_chip(d):
        return lax.rem(chip + d, CHIPS)

    def other_m(d):
        return lax.rem(me_m + d, mems)

    loads = [
        pltpu.make_async_copy(src, dst, load_sem.at[i])
        for i, (src, dst) in enumerate(
            (
                (perturb_hbm.at[:, 1 - core], perturb_raw.at[:, 1 - core]),
                (perturb_hbm.at[:, core], perturb_raw.at[:, core]),
                (coef_x_hbm.at[core], coef_x_raw),
                (coef_y_hbm.at[core], coef_y_raw),
            )
        )
    ]
    for copy in loads:
        copy.start()

    barrier = pltpu.get_barrier_semaphore()
    signal(sibling, me_t)

    @pl.loop(1, tiles)
    def _(d):
        t = lax.rem(me_t + d, tiles)
        signal(me_m, t)
        signal(sibling, t)

    @pl.loop(1, CHIPS)
    def _(d):
        m = 2 * other_chip(d) + core
        signal(m, me_t)
        signal(2 * other_chip(d) + 1 - core, me_t)
        signal(m, west)
        signal(m, east)

    with jax.named_scope("bucket"):
        tile = tile_ref[...]
        hot = jnp.concatenate([jnp.where(tile == t, 1.0, 0.0) for t in range(tiles)], axis=0)
        hot16 = hot.astype(BF16)
        lane_r, lane_c = iota((LANES, 2 * LANES), 0), iota((LANES, 2 * LANES), 1)
        earlier = jnp.where((lane_r < lane_c) | (lane_c >= LANES), 1.0, 0.0).astype(BF16)
        counts = dot(hot16, earlier, NN)
        rows = tiles * blocks
        row, col = iota((rows, rows), 0), iota((rows, rows), 1)
        before = (row // blocks == col // blocks) & (col < row)
        base = dot(jnp.where(before, 1.0, 0.0).astype(BF16), counts[:, LANES:].astype(BF16), NN)
        ranks = hot * (counts[:, :LANES] + base)
        rank = ranks[0:blocks]
        for t in range(1, tiles):
            rank = rank + ranks[t * blocks : (t + 1) * blocks]
        rank = rank.astype(I32)
        slot_row, slot_lane = tile * 8 + (rank >> 7), rank & 127
        cell = cell_ref[...]
        value_parts = split(values_ref[...])
        cell_parts = [(cell & mask).astype(F32) for mask in (0x7F, 0x7F << 7, 0x7 << 14)]
        sums = None
        for start in range(0, blocks, 4):
            left, right = [], []
            for b in range(start, start + 4):
                at = iota((8 * tiles, LANES), 0)
                here = at == slot_row[b : b + 1]
                there = at == slot_row[b : b + 1] + 3
                left.append(
                    jnp.concatenate(
                        [jnp.where(here, part[b : b + 1], 0.0) for part in value_parts]
                        + [jnp.where(there, part[b : b + 1], 0.0) for part in cell_parts],
                        axis=0,
                    ).astype(BF16)
                )
                right.append(jnp.where(iota((LANES, LANES), 0) == slot_lane[b : b + 1], 1.0, 0.0).astype(BF16))
            got = dot(jnp.concatenate(left, axis=1), jnp.concatenate(right, axis=1), NT)
            sums = got if sums is None else sums + got
        packed = sums[0 : 8 * tiles]
        for i in range(1, 5):
            packed = packed + sums[8 * tiles * i : 8 * tiles * (i + 1)]
        lists_out[...] = packed.reshape(tiles, 8, LANES)
    pl.semaphore_wait(barrier, 1 + 2 * (tiles - 1) + 4 * (CHIPS - 1))

    def list_copy(n, to):
        y, z = OFFSETS[n]
        t = lax.rem(me_t // DEPTH + y, 2) * DEPTH + lax.rem(me_t + DEPTH - z, DEPTH)
        return remote(
            lists_out.at[t], lists_in.at[2 * n + core], list_send.at[n, to], list_recv.at[2 * n + core],
            2 * chip + to, t,
        )

    to_sibling = remote(
        lists_out.at[me_t], lists_in.at[core], list_send.at[0, 0], list_recv.at[core], sibling, me_t
    )
    for n in range(tiles - 1, 0, -1):
        for to in range(2):
            list_copy(n, to).start()
    to_sibling.start()
    lists_in[core] = lists_out[me_t]

    to, source = iota((LAT, LAT), 0), iota((LAT, LAT), 1)
    order = jnp.where(source == (to % 8) * GROUPS + to // 8, 1.0, 0.0).astype(BF16)
    same = jnp.where(iota((LON, LON), 0) == iota((LON, LON), 1), 1.0, 0.0).astype(BF16)

    def ordered(l, f):
        side = jnp.concatenate([perturb_raw[k * FIELDS + f, l] for k in range(members)], axis=1)
        got = dot(order, side, NN)
        return [got[:, k * LON : (k + 1) * LON] for k in range(members)]

    def turn_in(i, x):
        turned = dot(same, x.astype(BF16), NT)
        for h in range(HALVES):
            perturb_t[i, h, HALO : HALO + LON] = turned[:, h * LANES : (h + 1) * LANES]

    share_copy = remote(perturb_out, perturb.at[pl.ds(own, own)], share_send.at[0], share_recv.at[0], sibling, me_t)
    loads[0].wait()
    with jax.named_scope("share"):
        for f in range(FIELDS):
            for k, x in enumerate(ordered(1 - core, f)):
                perturb_out[k * FIELDS + f] = x.reshape(GROUPS, 8, LANES)
    share_copy.start()
    for copy in loads[1:]:
        copy.wait()
    with jax.named_scope("prepare"):
        for f in range(FIELDS):
            for k, x in enumerate(ordered(core, f)):
                perturb[k * FIELDS + f] = x.reshape(GROUPS, 8, LANES)
                turn_in(k * FIELDS + f, x)

    with jax.named_scope("deposit"):
        total[...] = jnp.zeros_like(total)
        per_list = CAP // LANES
        span = 2

        @pl.loop(0, tiles // span)
        def _(i):
            for n in range(span):
                for c in range(2):
                    at = (i * span + n) * 2 + c

                    @pl.when(at != core)
                    def _():
                        remote(
                            lists_out.at[0], lists_in.at[at], list_send.at[0, 0], list_recv.at[at], sibling, me_t
                        ).wait_recv()

            lists = lists_in[pl.ds(i * 2 * span, 2 * span)]
            cells = lists.astype(I32)
            channel = cells >> 15
            grid_row = (((channel & 1) ^ core) << 10) | ((channel >> 1) << 7) | (cells & (LON - 1))
            grid_lane = (cells >> 7) & (LAT - 1)
            grid_lane = ((grid_lane & (GROUPS - 1)) << 3) | (grid_lane >> 5)
            high, low = split(lists)
            left, right = [], []
            for u in range(2 * span):
                for j in range(per_list):
                    here = iota((FIELDS * LON, LANES), 0) == grid_row[u, 3 + j : 4 + j]
                    left.append(jnp.where(here, 1.0, 0.0).astype(BF16))
                    here = iota((LAT, LANES), 0) == grid_lane[u, 3 + j : 4 + j]
                    right.append(
                        jnp.concatenate(
                            [
                                jnp.where(here, high[u, j : j + 1], 0.0).astype(BF16),
                                jnp.where(here, low[u, j : j + 1], 0.0).astype(BF16),
                            ],
                            axis=0,
                        )
                    )
            total[...] += dot(jnp.concatenate(left, axis=1), jnp.concatenate(right, axis=1), NT)

        for h in range(HALVES):
            lanes = slice(h * LANES, (h + 1) * LANES)
            lows = slice(LAT + h * LANES, LAT + (h + 1) * LANES)
            partial[h] = total[:, lanes] + total[:, lows]

    def rows(c):
        return pl.ds(pl.multiple_of(c * PART, PART), PART)

    def part_copy(d):
        c = other_chip(d)
        return remote(
            partial.at[:, rows(c)], partial_in.at[chip], part_send.at[d], part_recv.at[d], 2 * c + core, me_t
        )

    @pl.loop(1, CHIPS)
    def _(d):
        part_copy(d).start()

    share_copy.wait_recv()
    with jax.named_scope("prepare"):
        faces = []
        for b in range(GROUPS):
            faces.append(coef_x_raw[pl.ds(b, 8, stride=GROUPS), :])
            face = coef_y_raw[pl.ds(b, 8, stride=GROUPS), :]
            if b == GROUPS - 1:
                face = jnp.where(iota((8, LANES), 0) < 7, face, 0.0)
            coef_y[b] = face
        faces = jnp.concatenate(faces, axis=0)
        for h in range(HALVES):
            coef_t[h, HALO : HALO + LON] = faces[h * LANES : (h + 1) * LANES].T
        for i in range(own, 2 * own):
            turn_in(i, perturb[i].reshape(LAT, LANES))

    def at_p(start):
        return perturb_t.at[:, :, pl.ds(start, HALO)]

    def at_c(start):
        return coef_t.at[:, pl.ds(start, HALO)]

    edge_copies = []
    for i, at in enumerate((at_p, at_c)):
        edge_copies.append(remote(at(LON), at(0), edge_send.at[i, 0], edge_recv.at[i, 0], me_m, east))
        edge_copies.append(
            remote(at(HALO), at(HALO + LON), edge_send.at[i, 1], edge_recv.at[i, 1], me_m, west)
        )
    for copy in edge_copies:
        copy.start()

    def block(c):
        start = pl.multiple_of(HALO + lax.rem(c, 4) * PART, 8)
        return adjoint_t.at[c // 4, :, pl.ds(start, PART)]

    def add_part(d, acc):
        part_copy(d).wait_recv()
        return acc + partial_in[other_chip(CHIPS - d)]

    block(chip)[...] = lax.fori_loop(1, CHIPS, add_part, partial[:, rows(chip)])

    def adj_copy(d):
        mine = block(chip)
        return remote(mine, mine, adj_send.at[d], adj_recv.at[chip], 2 * other_chip(d) + core, me_t)

    def adj_from(c):
        there = block(c)
        return remote(there, there, adj_send.at[0], adj_recv.at[c], 2 * other_chip(1) + core, me_t)

    def halo_at(f, start):
        return adjoint_t.at[f, :, pl.ds(start, HALO)]

    def halo_copy(c, side):
        f = chip // 4
        source = halo_at(f, HALO if side else LON)
        target = halo_at(f, HALO + LON if side else 0)
        return remote(
            source, target, halo_send.at[c], halo_recv.at[f, side], 2 * c + core, west if side else east
        )

    def halo_from(f, side):
        target = halo_at(f, HALO + LON if side else 0)
        return remote(target, target, halo_send.at[0], halo_recv.at[f, side], me_m, east)

    for side in (0, 1):

        @pl.when(lax.rem(chip, 4) == (0 if side else 3))
        def _():
            @pl.loop(0, CHIPS)
            def _(c):
                halo_copy(c, side).start()

    @pl.loop(1, CHIPS)
    def _(d):
        adj_copy(d).start()

    for copy in edge_copies:
        copy.wait_recv()

    with jax.named_scope("gather"):

        @pl.loop(0, 2 * own)
        def _(i):
            for h in range(HALVES):
                for b in range(STEPS):
                    perturb_g[i, h, b] = perturb_t[i, h, pl.ds(b, 8, stride=STEPS), :]

        for h in range(HALVES):
            for b in range(STEPS):
                coef_g[h, b] = coef_t[h, pl.ds(b, 8, stride=STEPS), :]

    @pl.loop(1, CHIPS)
    def _(d):
        adj_from(other_chip(d)).wait_recv()

    for f in range(FIELDS):
        for side in (0, 1):
            halo_from(f, side).wait_recv()

    with jax.named_scope("east"):
        for f in range(FIELDS):
            for h in range(HALVES):
                for b in range(STEPS):
                    adjoint_g[f, h, b] = adjoint_t[f, h, pl.ds(b, 8, stride=STEPS), :]

        for h in range(HALVES):

            @pl.loop(0, 2 * members)
            def _(k):
                i = k * FIELDS
                v = [
                    perturb_g[i, h, b] * adjoint_g[0, h, b] + perturb_g[i + 1, h, b] * adjoint_g[1, h, b]
                    for b in range(STEPS)
                ]
                for _ in range(SWEEPS):
                    following = v[1:] + [pltpu.roll(v[0], 7, 0)]
                    flux = [coef_g[h, b] * (following[b] - v[b]) for b in range(STEPS)]
                    before = [pltpu.roll(flux[-1], 1, 0)] + flux[:-1]
                    v = [v[b] + flux[b] - before[b] for b in range(STEPS)]
                for b in range(STEPS):
                    diffused[k, h, pl.ds(b, 8, stride=STEPS), :] = v[b]

    with jax.named_scope("turn"):

        @pl.loop(0, members)
        def _(pair):
            for u in range(2):
                k = pair * 2 + u
                for h in range(HALVES):
                    turned = diffused[k, h, HALO : HALO + LON].T
                    half = GROUPS // HALVES
                    product[k, h * half : (h + 1) * half] = turned.reshape(half, 8, LANES)

    with jax.named_scope("north"):

        @pl.loop(0, 2 * members)
        def _(k):
            v = [product[k, b] for b in range(GROUPS)]
            for _ in range(SWEEPS):
                following = v[1:] + [pltpu.roll(v[0], 7, 0)]
                flux = [coef_y[b] * (following[b] - v[b]) for b in range(GROUPS)]
                before = [pltpu.roll(flux[-1], 1, 0)] + flux[:-1]
                v = [v[b] + flux[b] - before[b] for b in range(GROUPS)]
            for b in range(GROUPS):
                product[k, b] = v[b]

    share = LAT // mems

    with jax.named_scope("increments"):

        @pl.loop(0, GROUPS)
        def _(b):
            weights = [product[k, b] for k in range(2 * members)]
            for f in range(FIELDS):
                parts = [weights[k] * perturb[k * FIELDS + f, b] for k in range(2 * members)]
                while len(parts) > 1:
                    parts = [sum(parts[i : i + 2][1:], parts[i]) for i in range(0, len(parts), 2)]
                at = lax.rem(b, share) * 2 + f
                terms[b // share, pl.ds(at, 8, stride=2 * share), :] = parts[0]

    def out_rows(c):
        return pl.ds(pl.multiple_of(c * 2 * share, 2 * share), 2 * share)

    def term_copy(d):
        m = other_m(d)
        return remote(
            terms.at[lax.rem(m, 2), out_rows(m // 2)], terms_in.at[me_m], term_send.at[d], term_recv.at[d], m, me_t
        )

    @pl.loop(1, mems)
    def _(d):
        term_copy(d).start()

    terms_in[me_m] = terms[core, out_rows(chip)]

    @pl.loop(1, mems)
    def _(d):
        term_copy(d).wait_recv()

    for l in range(LEVELS):
        acc = terms_in[l]
        for c in range(1, CHIPS):
            acc = acc + terms_in[2 * c + l]
        out_ref[pl.ds(l, 2 * share, stride=LEVELS), :] = acc * (1.0 / (mems * members - 1))

    for copy in [to_sibling, share_copy] + edge_copies:
        copy.wait_send()

    for n in range(1, tiles):
        for to in range(2):
            list_copy(n, to).wait_send()

    @pl.loop(1, CHIPS)
    def _(d):
        part_copy(d).wait_send()
        adj_copy(d).wait_send()

    @pl.loop(1, mems)
    def _(d):
        term_copy(d).wait_send()

    for side in (0, 1):

        @pl.when(lax.rem(chip, 4) == (0 if side else 3))
        def _():
            @pl.loop(0, CHIPS)
            def _(c):
                halo_copy(c, side).wait_send()


def on_device(perturb, coef_x, coef_y, obs_values, obs_tile, obs_cell):
    tiles = lax.axis_size("tile")
    members = perturb.shape[0]
    own = members * FIELDS
    mems = 2 * CHIPS
    share = LAT // mems
    dma = pltpu.SemaphoreType.DMA

    def rows(*shape):
        return pltpu.VMEM((*shape, LANES), F32)

    out = pl.pallas_call(
        functools.partial(kernel, tiles=tiles, members=members),
        out_shape=jax.ShapeDtypeStruct((share * FIELDS * LEVELS, LANES), F32),
        in_specs=[pl.BlockSpec(memory_space=pl.ANY)] * 3 + [pl.BlockSpec(memory_space=pltpu.VMEM)] * 3,
        out_specs=pl.BlockSpec(memory_space=pltpu.VMEM),
        scratch_shapes=[
            pltpu.VMEM((own, LEVELS, LAT, LON), BF16),
            rows(LAT),
            rows(LAT),
            rows(2 * own, GROUPS, 8),
            rows(own, GROUPS, 8),
            rows(2 * own, HALVES, WIDE),
            rows(2 * own, HALVES, STEPS, 8),
            rows(HALVES, WIDE),
            rows(HALVES, STEPS, 8),
            rows(GROUPS, 8),
            rows(tiles, 8),
            rows(2 * tiles, 8),
            pltpu.VMEM((FIELDS * LON, 2 * LAT), F32),
            rows(HALVES, FIELDS * LON),
            rows(CHIPS, HALVES, PART),
            rows(FIELDS, HALVES, WIDE),
            rows(FIELDS, HALVES, STEPS, 8),
            rows(2 * members, HALVES, WIDE),
            rows(2 * members, GROUPS, 8),
            rows(2, LAT),
            rows(mems, 2 * share),
            dma((4,)),
            dma((tiles, 2)), dma((2 * tiles,)),
            dma((1,)), dma((1,)),
            dma((2, 2)), dma((2, 2)),
            dma((CHIPS,)), dma((CHIPS,)),
            dma((CHIPS,)), dma((CHIPS,)),
            dma((CHIPS,)), dma((FIELDS, 2)),
            dma((mems,)), dma((mems,)),
        ],
        compiler_params=pltpu.CompilerParams(
            collective_id=0, has_side_effects=True, vmem_limit_bytes=56 * 2**20
        ),
    )(
        perturb.reshape(own, LEVELS, LAT, LON),
        coef_x,
        coef_y,
        obs_values.reshape(-1, LANES),
        obs_tile.reshape(-1, LANES),
        obs_cell.reshape(-1, LANES),
    )
    return out.reshape(share, FIELDS, LEVELS, LANES)


def solution(mesh):
    return jax.shard_map(
        on_device,
        mesh=mesh,
        in_specs=(
            P("mem", None, None, None, "tile"),
            P(None, None, "tile"),
            P(None, None, "tile"),
            P(("mem", "tile")),
            P(("mem", "tile"), None),
            P(("mem", "tile")),
        ),
        out_specs=P("mem", None, None, "tile"),
        check_vma=False,
    )
```

```python
import functools

import jax
import jax.numpy as jnp
from jax import lax
from jax.experimental import pallas as pl
from jax.experimental.pallas import tpu as pltpu
from jax.sharding import PartitionSpec as P

FIELDS = 2
LEVELS = 2
SWEEPS = 6
LAT = 256
LON = 128
CAP = 384
LANES = 128
GROUPS = LAT // 8
HALO = 8
WIDE = LON + 2 * HALO
STEPS = WIDE // 8
HALVES = LAT // LANES
CHIPS = 8
DEPTH = 8
OFFSETS = ((0, 0), (0, 1), (0, 7), (0, 2), (0, 6), (1, 0), (0, 3), (0, 5), (1, 1), (1, 7), (0, 4), (1, 2), (1, 6), (1, 3), (1, 5), (1, 4))
PART = LON // 4
F32 = jnp.float32
BF16 = jnp.bfloat16
I32 = jnp.int32
NT = (((1,), (1,)), ((), ()))
NN = (((1,), (0,)), ((), ()))


def iota(shape, dim):
    return lax.broadcasted_iota(I32, shape, dim)


def dot(a, b, dims):
    return lax.dot_general(a, b, dims, preferred_element_type=F32)


def split(x):
    high = x.astype(BF16).astype(F32)
    return high, x - high


def kernel(
    perturb_hbm, coef_x_hbm, coef_y_hbm, values_ref, tile_ref, cell_ref, out_ref,
    perturb_raw, coef_x_raw, coef_y_raw, perturb, perturb_out, perturb_t, perturb_g, coef_t, coef_g, coef_y,
    lists_out, lists_in, total, partial, partial_in, adjoint_t, adjoint_g, diffused, product, terms, terms_in,
    load_sem, list_send, list_recv, share_send, share_recv, edge_send, edge_recv, part_send, part_recv,
    adj_send, adj_recv, halo_send, halo_recv, term_send, term_recv,
    *, tiles, members,
):
    me_m, me_t = lax.axis_index("mem"), lax.axis_index("tile")
    chip, core = me_m // 2, lax.rem(me_m, 2)
    sibling = 2 * chip + 1 - core
    west, east = lax.rem(me_t + tiles - 1, tiles), lax.rem(me_t + 1, tiles)
    blocks = values_ref.shape[0]
    mems = 2 * CHIPS
    own = members * FIELDS

    def remote(src, dst, send, recv, m, t):
        return pltpu.make_async_remote_copy(
            src_ref=src, dst_ref=dst, send_sem=send, recv_sem=recv,
            device_id={"mem": m, "tile": t}, device_id_type=pl.DeviceIdType.MESH,
        )

    def signal(m, t):
        pl.semaphore_signal(
            barrier, 1, device_id={"mem": m, "tile": t}, device_id_type=pl.DeviceIdType.MESH
        )

    def other_chip(d):
        return lax.rem(chip + d, CHIPS)

    def other_m(d):
        return lax.rem(me_m + d, mems)

    loads = [
        pltpu.make_async_copy(src, dst, load_sem.at[i])
        for i, (src, dst) in enumerate(
            (
                (perturb_hbm.at[:, 1 - core], perturb_raw.at[:, 1 - core]),
                (perturb_hbm.at[:, core], perturb_raw.at[:, core]),
                (coef_x_hbm.at[core], coef_x_raw),
                (coef_y_hbm.at[core], coef_y_raw),
            )
        )
    ]
    for copy in loads:
        copy.start()

    barrier = pltpu.get_barrier_semaphore()
    signal(sibling, me_t)

    @pl.loop(1, tiles)
    def _(d):
        t = lax.rem(me_t + d, tiles)
        signal(me_m, t)
        signal(sibling, t)

    @pl.loop(1, CHIPS)
    def _(d):
        m = 2 * other_chip(d) + core
        signal(m, me_t)
        signal(2 * other_chip(d) + 1 - core, me_t)
        signal(m, west)
        signal(m, east)

    with jax.named_scope("bucket"):
        tile = tile_ref[...]
        hot = jnp.concatenate([jnp.where(tile == t, 1.0, 0.0) for t in range(tiles)], axis=0)
        hot16 = hot.astype(BF16)
        lane_r, lane_c = iota((LANES, 2 * LANES), 0), iota((LANES, 2 * LANES), 1)
        earlier = jnp.where((lane_r < lane_c) | (lane_c >= LANES), 1.0, 0.0).astype(BF16)
        counts = dot(hot16, earlier, NN)
        rows = tiles * blocks
        row, col = iota((rows, rows), 0), iota((rows, rows), 1)
        before = (row // blocks == col // blocks) & (col < row)
        base = dot(jnp.where(before, 1.0, 0.0).astype(BF16), counts[:, LANES:].astype(BF16), NN)
        ranks = hot * (counts[:, :LANES] + base)
        rank = ranks[0:blocks]
        for t in range(1, tiles):
            rank = rank + ranks[t * blocks : (t + 1) * blocks]
        rank = rank.astype(I32)
        slot_row, slot_lane = tile * 8 + (rank >> 7), rank & 127
        cell = cell_ref[...]
        value_parts = split(values_ref[...])
        cell_parts = [(cell & mask).astype(F32) for mask in (0x7F, 0x7F << 7, 0x7 << 14)]
        sums = None
        for start in range(0, blocks, 4):
            left, right = [], []
            for b in range(start, start + 4):
                at = iota((8 * tiles, LANES), 0)
                here = at == slot_row[b : b + 1]
                there = at == slot_row[b : b + 1] + 3
                left.append(
                    jnp.concatenate(
                        [jnp.where(here, part[b : b + 1], 0.0) for part in value_parts]
                        + [jnp.where(there, part[b : b + 1], 0.0) for part in cell_parts],
                        axis=0,
                    ).astype(BF16)
                )
                right.append(jnp.where(iota((LANES, LANES), 0) == slot_lane[b : b + 1], 1.0, 0.0).astype(BF16))
            got = dot(jnp.concatenate(left, axis=1), jnp.concatenate(right, axis=1), NT)
            sums = got if sums is None else sums + got
        packed = sums[0 : 8 * tiles]
        for i in range(1, 5):
            packed = packed + sums[8 * tiles * i : 8 * tiles * (i + 1)]
        lists_out[...] = packed.reshape(tiles, 8, LANES)
    pl.semaphore_wait(barrier, 1 + 2 * (tiles - 1) + 4 * (CHIPS - 1))

    def list_copy(n, to):
        y, z = OFFSETS[n]
        t = lax.rem(me_t // DEPTH + y, 2) * DEPTH + lax.rem(me_t + DEPTH - z, DEPTH)
        return remote(
            lists_out.at[t], lists_in.at[2 * n + core], list_send.at[n, to], list_recv.at[2 * n + core],
            2 * chip + to, t,
        )

    to_sibling = remote(
        lists_out.at[me_t], lists_in.at[core], list_send.at[0, 0], list_recv.at[core], sibling, me_t
    )
    for n in range(tiles - 1, 0, -1):
        for to in range(2):
            list_copy(n, to).start()
    to_sibling.start()
    lists_in[core] = lists_out[me_t]

    to, source = iota((LAT, LAT), 0), iota((LAT, LAT), 1)
    order = jnp.where(source == (to % 8) * GROUPS + to // 8, 1.0, 0.0).astype(BF16)
    same = jnp.where(iota((LON, LON), 0) == iota((LON, LON), 1), 1.0, 0.0).astype(BF16)

    def ordered(l, f):
        side = jnp.concatenate([perturb_raw[k * FIELDS + f, l] for k in range(members)], axis=1)
        got = dot(order, side, NN)
        return [got[:, k * LON : (k + 1) * LON] for k in range(members)]

    def turn_in(i, x):
        turned = dot(same, x.astype(BF16), NT)
        for h in range(HALVES):
            perturb_t[i, h, HALO : HALO + LON] = turned[:, h * LANES : (h + 1) * LANES]

    share_copy = remote(perturb_out, perturb.at[pl.ds(own, own)], share_send.at[0], share_recv.at[0], sibling, me_t)
    loads[0].wait()
    with jax.named_scope("share"):
        for f in range(FIELDS):
            for k, x in enumerate(ordered(1 - core, f)):
                perturb_out[k * FIELDS + f] = x.reshape(GROUPS, 8, LANES)
    share_copy.start()
    for copy in loads[1:]:
        copy.wait()
    with jax.named_scope("prepare"):
        for f in range(FIELDS):
            for k, x in enumerate(ordered(core, f)):
                perturb[k * FIELDS + f] = x.reshape(GROUPS, 8, LANES)
                turn_in(k * FIELDS + f, x)
        faces = []
        for b in range(GROUPS):
            faces.append(coef_x_raw[pl.ds(b, 8, stride=GROUPS), :])
            face = coef_y_raw[pl.ds(b, 8, stride=GROUPS), :]
            if b == GROUPS - 1:
                face = jnp.where(iota((8, LANES), 0) < 7, face, 0.0)
            coef_y[b] = face
        faces = jnp.concatenate(faces, axis=0)
        for h in range(HALVES):
            coef_t[h, HALO : HALO + LON] = faces[h * LANES : (h + 1) * LANES].T

    def edges_of(start):
        mine, theirs = pl.ds(0, own), pl.ds(own, own)
        at = pl.ds(start, HALO)
        return coef_t.at[:, at], perturb_t.at[mine, :, at], perturb_t.at[theirs, :, at]

    edge_copies = []
    for i in range(3):
        edge_copies.append(
            remote(edges_of(LON)[i], edges_of(0)[i], edge_send.at[i, 0], edge_recv.at[i, 0], me_m, east)
        )
        edge_copies.append(
            remote(edges_of(HALO)[i], edges_of(HALO + LON)[i], edge_send.at[i, 1], edge_recv.at[i, 1], me_m, west)
        )
    for copy in edge_copies[:4]:
        copy.start()

    with jax.named_scope("deposit"):
        total[...] = jnp.zeros_like(total)
        counting = (iota((LAT // 16, 16, LANES), 0) * 16 + iota((LAT // 16, 16, LANES), 1)).astype(F32).astype(BF16)
        one, zero = jnp.ones((), BF16), jnp.zeros((), BF16)

        def repeated(x):
            return jnp.broadcast_to(x, (16, LANES)).astype(BF16)[None]

        per_list = CAP // LANES
        span = 4

        @pl.loop(0, tiles // span)
        def _(i):
            for n in range(span):
                for c in range(2):
                    at = (i * span + n) * 2 + c

                    @pl.when(at != core)
                    def _():
                        remote(
                            lists_out.at[0], lists_in.at[at], list_send.at[0, 0], list_recv.at[at], sibling, me_t
                        ).wait_recv()

            lists = lists_in[pl.ds(i * 2 * span, 2 * span)]
            cells = lists.astype(I32)
            channel = cells >> 15
            grid_row = (((channel & 1) ^ core) << 10) | ((channel >> 1) << 7) | (cells & (LON - 1))
            grid_lane = (cells >> 7) & (LAT - 1)
            grid_lane = ((grid_lane & (GROUPS - 1)) << 3) | (grid_lane >> 5)
            high, low = split(lists)
            left, right = [], []
            for u in range(2 * span):
                for j in range(per_list):
                    here = counting == repeated(grid_lane.astype(F32)[u, 3 + j : 4 + j])
                    right.append(jnp.where(here, one, zero).reshape(LAT, LANES))
                    here = counting == repeated(grid_row.astype(F32)[u, 3 + j : 4 + j])
                    left.append(
                        jnp.concatenate(
                            [
                                jnp.where(here, repeated(part[u, j : j + 1]), zero).reshape(LAT, LANES)
                                for part in (high, low)
                            ],
                            axis=0,
                        )
                    )
            total[...] += dot(jnp.concatenate(left, axis=1), jnp.concatenate(right, axis=1), NT)

        for h in range(HALVES):
            lanes = slice(h * LANES, (h + 1) * LANES)
            partial[h] = total[: FIELDS * LON, lanes] + total[FIELDS * LON :, lanes]

    def rows(c):
        return pl.ds(pl.multiple_of(c * PART, PART), PART)

    def part_copy(d):
        c = other_chip(d)
        return remote(
            partial.at[:, rows(c)], partial_in.at[chip], part_send.at[d], part_recv.at[d], 2 * c + core, me_t
        )

    @pl.loop(1, CHIPS)
    def _(d):
        part_copy(d).start()

    share_copy.wait_recv()
    with jax.named_scope("prepare"):
        for i in range(own, 2 * own):
            turn_in(i, perturb[i].reshape(LAT, LANES))

    for copy in edge_copies[4:]:
        copy.start()

    def block(c):
        start = pl.multiple_of(HALO + lax.rem(c, 4) * PART, 8)
        return adjoint_t.at[c // 4, :, pl.ds(start, PART)]

    def add_part(d, acc):
        part_copy(d).wait_recv()
        return acc + partial_in[other_chip(CHIPS - d)]

    block(chip)[...] = lax.fori_loop(1, CHIPS, add_part, partial[:, rows(chip)])

    def adj_copy(d):
        mine = block(chip)
        return remote(mine, mine, adj_send.at[d], adj_recv.at[chip], 2 * other_chip(d) + core, me_t)

    def adj_from(c):
        there = block(c)
        return remote(there, there, adj_send.at[0], adj_recv.at[c], 2 * other_chip(1) + core, me_t)

    def halo_at(f, start):
        return adjoint_t.at[f, :, pl.ds(start, HALO)]

    def halo_copy(c, side):
        f = chip // 4
        source = halo_at(f, HALO if side else LON)
        target = halo_at(f, HALO + LON if side else 0)
        return remote(
            source, target, halo_send.at[c], halo_recv.at[f, side], 2 * c + core, west if side else east
        )

    def halo_from(f, side):
        target = halo_at(f, HALO + LON if side else 0)
        return remote(target, target, halo_send.at[0], halo_recv.at[f, side], me_m, east)

    for side in (0, 1):

        @pl.when(lax.rem(chip, 4) == (0 if side else 3))
        def _():
            @pl.loop(0, CHIPS)
            def _(c):
                halo_copy(c, side).start()

    @pl.loop(1, CHIPS)
    def _(d):
        adj_copy(d).start()

    for copy in edge_copies:
        copy.wait_recv()

    with jax.named_scope("gather"):

        @pl.loop(0, 2 * own)
        def _(i):
            for h in range(HALVES):
                for b in range(STEPS):
                    perturb_g[i, h, b] = perturb_t[i, h, pl.ds(b, 8, stride=STEPS), :]

        for h in range(HALVES):
            for b in range(STEPS):
                coef_g[h, b] = coef_t[h, pl.ds(b, 8, stride=STEPS), :]

    @pl.loop(1, CHIPS)
    def _(d):
        adj_from(other_chip(d)).wait_recv()

    for f in range(FIELDS):
        for side in (0, 1):
            halo_from(f, side).wait_recv()

    with jax.named_scope("east"):
        for f in range(FIELDS):
            for h in range(HALVES):
                for b in range(STEPS):
                    adjoint_g[f, h, b] = adjoint_t[f, h, pl.ds(b, 8, stride=STEPS), :]

        @pl.loop(0, 2 * members)
        def _(k):
            i = k * FIELDS
            places = [(h, b) for h in range(HALVES) for b in range(STEPS)]
            v = {
                p: perturb_g[i, *p] * adjoint_g[0, *p] + perturb_g[i + 1, *p] * adjoint_g[1, *p]
                for p in places
            }
            for _ in range(SWEEPS):
                end = [pltpu.roll(v[h, 0], 7, 0) for h in range(HALVES)]
                flux = {
                    (h, b): coef_g[h, b] * ((v[h, b + 1] if b + 1 < STEPS else end[h]) - v[h, b])
                    for h, b in places
                }
                start = [pltpu.roll(flux[h, STEPS - 1], 1, 0) for h in range(HALVES)]
                v = {
                    (h, b): v[h, b] + flux[h, b] - (flux[h, b - 1] if b else start[h])
                    for h, b in places
                }
            for h, b in places:
                diffused[k, h, pl.ds(b, 8, stride=STEPS), :] = v[h, b]

    with jax.named_scope("turn"):
        twice = jnp.where((iota((LAT, 2 * LAT), 1) & (LAT - 1)) == iota((LAT, 2 * LAT), 0), 1.0, 0.0).astype(BF16)
        for pair in range(members):
            sides = []
            for k in (2 * pair, 2 * pair + 1):
                parts = [split(diffused[k, h, HALO : HALO + LON]) for h in range(HALVES)]
                sides.append(jnp.concatenate([p[i] for i in range(2) for p in parts], axis=1).astype(BF16))
            turned = dot(twice, jnp.concatenate(sides, axis=0), NT)
            for u in range(2):
                product[2 * pair + u] = turned[:, u * LON : (u + 1) * LON].reshape(GROUPS, 8, LANES)

    with jax.named_scope("north"):

        @pl.loop(0, 2 * members)
        def _(k):
            v = [product[k, b] for b in range(GROUPS)]
            for _ in range(SWEEPS):
                following = v[1:] + [pltpu.roll(v[0], 7, 0)]
                flux = [coef_y[b] * (following[b] - v[b]) for b in range(GROUPS)]
                before = [pltpu.roll(flux[-1], 1, 0)] + flux[:-1]
                v = [v[b] + flux[b] - before[b] for b in range(GROUPS)]
            for b in range(GROUPS):
                product[k, b] = v[b]

    share = LAT // mems

    def out_rows(c):
        return pl.ds(pl.multiple_of(c * 2 * share, 2 * share), 2 * share)

    def term_copy(to, d):
        c = other_chip(d)
        return remote(
            terms.at[to, out_rows(c)], terms_in.at[me_m], term_send.at[to, c], term_recv.at[me_m], 2 * c + to, me_t
        )

    def increments(half):
        @pl.loop(0, share, unroll=4)
        def _(b):
            at = half * share + b
            weights = [product[k, at] for k in range(2 * members)]
            for f in range(FIELDS):
                parts = [weights[k] * perturb[k * FIELDS + f, at] for k in range(2 * members)]
                while len(parts) > 1:
                    parts = [sum(parts[i : i + 2][1:], parts[i]) for i in range(0, len(parts), 2)]
                terms[half, pl.ds(2 * b + f, 8, stride=2 * share), :] = parts[0]

    with jax.named_scope("increments"):
        increments(1 - core)

    @pl.loop(0, CHIPS)
    def _(d):
        term_copy(1 - core, d).start()

    with jax.named_scope("increments"):
        increments(core)

    @pl.loop(1, CHIPS)
    def _(d):
        term_copy(core, d).start()

    terms_in[me_m] = terms[core, out_rows(chip)]

    @pl.loop(1, mems)
    def _(d):
        m = other_m(d)
        remote(terms_in.at[m], terms_in.at[m], term_send.at[0, 0], term_recv.at[m], sibling, me_t).wait_recv()

    for l in range(LEVELS):
        acc = terms_in[l]
        for c in range(1, CHIPS):
            acc = acc + terms_in[2 * c + l]
        out_ref[pl.ds(l, 2 * share, stride=LEVELS), :] = acc * (1.0 / (mems * members - 1))

    for copy in [to_sibling, share_copy] + edge_copies:
        copy.wait_send()

    for n in range(1, tiles):
        for to in range(2):
            list_copy(n, to).wait_send()

    @pl.loop(1, CHIPS)
    def _(d):
        part_copy(d).wait_send()
        adj_copy(d).wait_send()
        term_copy(core, d).wait_send()

    @pl.loop(0, CHIPS)
    def _(d):
        term_copy(1 - core, d).wait_send()

    for side in (0, 1):

        @pl.when(lax.rem(chip, 4) == (0 if side else 3))
        def _():
            @pl.loop(0, CHIPS)
            def _(c):
                halo_copy(c, side).wait_send()


def on_device(perturb, coef_x, coef_y, obs_values, obs_tile, obs_cell):
    tiles = lax.axis_size("tile")
    members = perturb.shape[0]
    own = members * FIELDS
    mems = 2 * CHIPS
    share = LAT // mems
    dma = pltpu.SemaphoreType.DMA

    def rows(*shape):
        return pltpu.VMEM((*shape, LANES), F32)

    out = pl.pallas_call(
        functools.partial(kernel, tiles=tiles, members=members),
        out_shape=jax.ShapeDtypeStruct((share * FIELDS * LEVELS, LANES), F32),
        in_specs=[pl.BlockSpec(memory_space=pl.ANY)] * 3 + [pl.BlockSpec(memory_space=pltpu.VMEM)] * 3,
        out_specs=pl.BlockSpec(memory_space=pltpu.VMEM),
        scratch_shapes=[
            pltpu.VMEM((own, LEVELS, LAT, LON), BF16),
            rows(LAT),
            rows(LAT),
            rows(2 * own, GROUPS, 8),
            rows(own, GROUPS, 8),
            rows(2 * own, HALVES, WIDE),
            rows(2 * own, HALVES, STEPS, 8),
            rows(HALVES, WIDE),
            rows(HALVES, STEPS, 8),
            rows(GROUPS, 8),
            rows(tiles, 8),
            rows(2 * tiles, 8),
            pltpu.VMEM((2 * FIELDS * LON, LAT), F32),
            rows(HALVES, FIELDS * LON),
            rows(CHIPS, HALVES, PART),
            rows(FIELDS, HALVES, WIDE),
            rows(FIELDS, HALVES, STEPS, 8),
            rows(2 * members, HALVES, WIDE),
            rows(2 * members, GROUPS, 8),
            rows(2, LAT),
            rows(mems, 2 * share),
            dma((4,)),
            dma((tiles, 2)), dma((2 * tiles,)),
            dma((1,)), dma((1,)),
            dma((3, 2)), dma((3, 2)),
            dma((CHIPS,)), dma((CHIPS,)),
            dma((CHIPS,)), dma((CHIPS,)),
            dma((CHIPS,)), dma((FIELDS, 2)),
            dma((2, CHIPS)), dma((mems,)),
        ],
        compiler_params=pltpu.CompilerParams(
            collective_id=0, has_side_effects=True, vmem_limit_bytes=56 * 2**20
        ),
    )(
        perturb.reshape(own, LEVELS, LAT, LON),
        coef_x,
        coef_y,
        obs_values.reshape(-1, LANES),
        obs_tile.reshape(-1, LANES),
        obs_cell.reshape(-1, LANES),
    )
    return out.reshape(share, FIELDS, LEVELS, LANES)


def solution(mesh):
    return jax.shard_map(
        on_device,
        mesh=mesh,
        in_specs=(
            P("mem", None, None, None, "tile"),
            P(None, None, "tile"),
            P(None, None, "tile"),
            P(("mem", "tile")),
            P(("mem", "tile"), None),
            P(("mem", "tile")),
        ),
        out_specs=P("mem", None, None, "tile"),
        check_vma=False,
    )
```

```python
import functools

import jax
import jax.numpy as jnp
from jax import lax
from jax.experimental import pallas as pl
from jax.experimental.pallas import tpu as pltpu
from jax.sharding import PartitionSpec as P

FIELDS = 2
LEVELS = 2
SWEEPS = 6
LAT = 256
LON = 128
CAP = 384
LANES = 128
GROUPS = LAT // 8
HALO = 8
WIDE = LON + 2 * HALO
STEPS = WIDE // 8
HALVES = LAT // LANES
CHIPS = 8
DEPTH = 8
OFFSETS = ((0, 0), (0, 1), (0, 7), (0, 2), (0, 6), (1, 0), (0, 3), (0, 5), (1, 1), (1, 7), (0, 4), (1, 2), (1, 6), (1, 3), (1, 5), (1, 4))
PART = LON // 4
F32 = jnp.float32
BF16 = jnp.bfloat16
I32 = jnp.int32
NT = (((1,), (1,)), ((), ()))
NN = (((1,), (0,)), ((), ()))


def iota(shape, dim):
    return lax.broadcasted_iota(I32, shape, dim)


def dot(a, b, dims):
    return lax.dot_general(a, b, dims, preferred_element_type=F32)


def split(x):
    high = x.astype(BF16).astype(F32)
    return high, x - high


def kernel(
    perturb_hbm, coef_x_hbm, coef_y_hbm, values_ref, tile_ref, cell_ref, out_ref,
    perturb_raw, coef_x_raw, coef_y_raw, perturb, perturb_out, perturb_t, perturb_g, coef_t, coef_g, coef_y,
    lists_out, lists_in, total, partial, partial_in, adjoint_t, adjoint_g, diffused, product, terms, terms_in,
    load_sem, list_send, list_recv, share_send, share_recv, edge_send, edge_recv, part_send, part_recv,
    adj_send, adj_recv, halo_send, halo_recv, term_send, term_recv,
    *, tiles, members,
):
    me_m, me_t = lax.axis_index("mem"), lax.axis_index("tile")
    chip, core = me_m // 2, lax.rem(me_m, 2)
    sibling = 2 * chip + 1 - core
    west, east = lax.rem(me_t + tiles - 1, tiles), lax.rem(me_t + 1, tiles)
    blocks = values_ref.shape[0]
    mems = 2 * CHIPS
    own = members * FIELDS

    def remote(src, dst, send, recv, m, t):
        return pltpu.make_async_remote_copy(
            src_ref=src, dst_ref=dst, send_sem=send, recv_sem=recv,
            device_id={"mem": m, "tile": t}, device_id_type=pl.DeviceIdType.MESH,
        )

    def signal(m, t):
        pl.semaphore_signal(
            barrier, 1, device_id={"mem": m, "tile": t}, device_id_type=pl.DeviceIdType.MESH
        )

    def other_chip(d):
        return lax.rem(chip + d, CHIPS)

    order7 = [lax.rem(chip // 4 + y, 2) * 4 + lax.rem(lax.rem(chip, 4) + x, 4) for y, x in ((1, 2), (1, 1), (1, 3), (0, 2), (1, 0), (0, 1), (0, 3))]

    def other_m(d):
        return lax.rem(me_m + d, mems)

    loads = [
        pltpu.make_async_copy(src, dst, load_sem.at[i])
        for i, (src, dst) in enumerate(
            (
                (perturb_hbm.at[:, 1 - core], perturb_raw.at[:, 1 - core]),
                (perturb_hbm.at[:, core], perturb_raw.at[:, core]),
                (coef_x_hbm.at[core], coef_x_raw),
                (coef_y_hbm.at[core], coef_y_raw),
            )
        )
    ]
    for copy in loads:
        copy.start()

    barrier = pltpu.get_barrier_semaphore()
    signal(sibling, me_t)

    @pl.loop(1, tiles)
    def _(d):
        t = lax.rem(me_t + d, tiles)
        signal(me_m, t)
        signal(sibling, t)

    @pl.loop(1, CHIPS)
    def _(d):
        m = 2 * other_chip(d) + core
        signal(m, me_t)
        signal(2 * other_chip(d) + 1 - core, me_t)
        signal(m, west)
        signal(m, east)

    with jax.named_scope("bucket"):
        tile = tile_ref[...]
        hot = jnp.concatenate([jnp.where(tile == t, 1.0, 0.0) for t in range(tiles)], axis=0)
        hot16 = hot.astype(BF16)
        lane_r, lane_c = iota((LANES, 2 * LANES), 0), iota((LANES, 2 * LANES), 1)
        earlier = jnp.where((lane_r < lane_c) | (lane_c >= LANES), 1.0, 0.0).astype(BF16)
        counts = dot(hot16, earlier, NN)
        rows = tiles * blocks
        row, col = iota((rows, rows), 0), iota((rows, rows), 1)
        before = (row // blocks == col // blocks) & (col < row)
        base = dot(jnp.where(before, 1.0, 0.0).astype(BF16), counts[:, LANES:].astype(BF16), NN)
        ranks = hot * (counts[:, :LANES] + base)
        rank = ranks[0:blocks]
        for t in range(1, tiles):
            rank = rank + ranks[t * blocks : (t + 1) * blocks]
        rank = rank.astype(I32)
        slot_row, slot_lane = tile * 8 + (rank >> 7), rank & 127
        cell = cell_ref[...]
        value_parts = split(values_ref[...])
        cell_parts = [(cell & mask).astype(F32) for mask in (0x7F, 0x7F << 7, 0x7 << 14)]
        sums = None
        for start in range(0, blocks, 4):
            left, right = [], []
            for b in range(start, start + 4):
                at = iota((8 * tiles, LANES), 0)
                here = at == slot_row[b : b + 1]
                there = at == slot_row[b : b + 1] + 3
                left.append(
                    jnp.concatenate(
                        [jnp.where(here, part[b : b + 1], 0.0) for part in value_parts]
                        + [jnp.where(there, part[b : b + 1], 0.0) for part in cell_parts],
                        axis=0,
                    ).astype(BF16)
                )
                right.append(jnp.where(iota((LANES, LANES), 0) == slot_lane[b : b + 1], 1.0, 0.0).astype(BF16))
            got = dot(jnp.concatenate(left, axis=1), jnp.concatenate(right, axis=1), NT)
            sums = got if sums is None else sums + got
        packed = sums[0 : 8 * tiles]
        for i in range(1, 5):
            packed = packed + sums[8 * tiles * i : 8 * tiles * (i + 1)]
        lists_out[...] = packed.reshape(tiles, 8, LANES)
    pl.semaphore_wait(barrier, 1 + 2 * (tiles - 1) + 4 * (CHIPS - 1))

    def list_copy(n, to):
        y, z = OFFSETS[n]
        t = lax.rem(me_t // DEPTH + y, 2) * DEPTH + lax.rem(me_t + DEPTH - z, DEPTH)
        return remote(
            lists_out.at[t], lists_in.at[2 * n + core], list_send.at[n, to], list_recv.at[2 * n + core],
            2 * chip + to, t,
        )

    to_sibling = remote(
        lists_out.at[me_t], lists_in.at[core], list_send.at[0, 0], list_recv.at[core], sibling, me_t
    )
    for n in range(tiles - 1, 0, -1):
        for to in range(2):
            list_copy(n, to).start()
    to_sibling.start()
    lists_in[core] = lists_out[me_t]

    to, source = iota((LAT, LAT), 0), iota((LAT, LAT), 1)
    order = jnp.where(source == (to % 8) * GROUPS + to // 8, 1.0, 0.0).astype(BF16)
    same = jnp.where(iota((LON, LON), 0) == iota((LON, LON), 1), 1.0, 0.0).astype(BF16)

    def ordered(l, f):
        side = jnp.concatenate([perturb_raw[k * FIELDS + f, l] for k in range(members)], axis=1)
        got = dot(order, side, NN)
        return [got[:, k * LON : (k + 1) * LON] for k in range(members)]

    def turn_in(i, x):
        turned = dot(same, x.astype(BF16), NT)
        for h in range(HALVES):
            perturb_t[i, h, HALO : HALO + LON] = turned[:, h * LANES : (h + 1) * LANES]

    share_copy = remote(perturb_out, perturb.at[pl.ds(own, own)], share_send.at[0], share_recv.at[0], sibling, me_t)
    loads[0].wait()
    with jax.named_scope("share"):
        for f in range(FIELDS):
            for k, x in enumerate(ordered(1 - core, f)):
                perturb_out[k * FIELDS + f] = x.reshape(GROUPS, 8, LANES)
    share_copy.start()
    for copy in loads[1:]:
        copy.wait()
    with jax.named_scope("prepare"):
        for f in range(FIELDS):
            for k, x in enumerate(ordered(core, f)):
                perturb[k * FIELDS + f] = x.reshape(GROUPS, 8, LANES)
                turn_in(k * FIELDS + f, x)
        faces = []
        for b in range(GROUPS):
            faces.append(coef_x_raw[pl.ds(b, 8, stride=GROUPS), :])
            face = coef_y_raw[pl.ds(b, 8, stride=GROUPS), :]
            if b == GROUPS - 1:
                face = jnp.where(iota((8, LANES), 0) < 7, face, 0.0)
            coef_y[b] = face
        faces = jnp.concatenate(faces, axis=0)
        for h in range(HALVES):
            coef_t[h, HALO : HALO + LON] = faces[h * LANES : (h + 1) * LANES].T

    def edges_of(start):
        mine, theirs = pl.ds(0, own), pl.ds(own, own)
        at = pl.ds(start, HALO)
        return coef_t.at[:, at], perturb_t.at[mine, :, at], perturb_t.at[theirs, :, at]

    edge_copies = []
    for i in range(3):
        edge_copies.append(
            remote(edges_of(LON)[i], edges_of(0)[i], edge_send.at[i, 0], edge_recv.at[i, 0], me_m, east)
        )
        edge_copies.append(
            remote(edges_of(HALO)[i], edges_of(HALO + LON)[i], edge_send.at[i, 1], edge_recv.at[i, 1], me_m, west)
        )
    for copy in edge_copies[:4]:
        copy.start()

    share_copy.wait_recv()
    with jax.named_scope("prepare"):
        for i in range(own, 2 * own):
            turn_in(i, perturb[i].reshape(LAT, LANES))

    for copy in edge_copies[4:]:
        copy.start()

    with jax.named_scope("deposit"):
        total[...] = jnp.zeros_like(total)
        counting = (iota((LAT // 16, 16, LANES), 0) * 16 + iota((LAT // 16, 16, LANES), 1)).astype(F32).astype(BF16)
        one, zero = jnp.ones((), BF16), jnp.zeros((), BF16)

        def repeated(x):
            return jnp.broadcast_to(x, (16, LANES)).astype(BF16)[None]

        per_list = CAP // LANES
        span = 4

        @pl.loop(0, tiles // span)
        def _(i):
            for n in range(span):
                for c in range(2):
                    at = (i * span + n) * 2 + c

                    @pl.when(at != core)
                    def _():
                        remote(
                            lists_out.at[0], lists_in.at[at], list_send.at[0, 0], list_recv.at[at], sibling, me_t
                        ).wait_recv()

            lists = lists_in[pl.ds(i * 2 * span, 2 * span)]
            cells = lists.astype(I32)
            channel = cells >> 15
            grid_row = (((channel & 1) ^ core) << 10) | ((channel >> 1) << 7) | (cells & (LON - 1))
            grid_lane = (cells >> 7) & (LAT - 1)
            grid_lane = ((grid_lane & (GROUPS - 1)) << 3) | (grid_lane >> 5)
            high, low = split(lists)
            left, right = [], []
            for u in range(2 * span):
                for j in range(per_list):
                    here = counting == repeated(grid_lane.astype(F32)[u, 3 + j : 4 + j])
                    right.append(jnp.where(here, one, zero).reshape(LAT, LANES))
                    here = counting == repeated(grid_row.astype(F32)[u, 3 + j : 4 + j])
                    left.append(
                        jnp.concatenate(
                            [
                                jnp.where(here, repeated(part[u, j : j + 1]), zero).reshape(LAT, LANES)
                                for part in (high, low)
                            ],
                            axis=0,
                        )
                    )
            total[...] += dot(jnp.concatenate(left, axis=1), jnp.concatenate(right, axis=1), NT)

        for h in range(HALVES):
            lanes = slice(h * LANES, (h + 1) * LANES)
            partial[h] = total[: FIELDS * LON, lanes] + total[FIELDS * LON :, lanes]

    def rows(c):
        return pl.ds(pl.multiple_of(c * PART, PART), PART)

    def part_copy(d):
        c = other_chip(d)
        return remote(
            partial.at[:, rows(c)], partial_in.at[chip], part_send.at[d], part_recv.at[d], 2 * c + core, me_t
        )

    for c in order7:
        part_copy(lax.rem(c - chip + CHIPS, CHIPS)).start()

    def block(c):
        start = pl.multiple_of(HALO + lax.rem(c, 4) * PART, 8)
        return adjoint_t.at[c // 4, :, pl.ds(start, PART)]

    def add_part(d, acc):
        part_copy(d).wait_recv()
        return acc + partial_in[other_chip(CHIPS - d)]

    block(chip)[...] = lax.fori_loop(1, CHIPS, add_part, partial[:, rows(chip)])

    def adj_copy(d):
        mine = block(chip)
        return remote(mine, mine, adj_send.at[d], adj_recv.at[chip], 2 * other_chip(d) + core, me_t)

    def adj_from(c):
        there = block(c)
        return remote(there, there, adj_send.at[0], adj_recv.at[c], 2 * other_chip(1) + core, me_t)

    def halo_at(f, start):
        return adjoint_t.at[f, :, pl.ds(start, HALO)]

    def halo_copy(c, side):
        f = chip // 4
        source = halo_at(f, HALO if side else LON)
        target = halo_at(f, HALO + LON if side else 0)
        return remote(
            source, target, halo_send.at[c], halo_recv.at[f, side], 2 * c + core, west if side else east
        )

    def halo_from(f, side):
        target = halo_at(f, HALO + LON if side else 0)
        return remote(target, target, halo_send.at[0], halo_recv.at[f, side], me_m, east)

    for side in (0, 1):

        @pl.when(lax.rem(chip, 4) == (0 if side else 3))
        def _():
            @pl.loop(0, CHIPS)
            def _(c):
                halo_copy(c, side).start()

    for c in order7:
        adj_copy(lax.rem(c - chip + CHIPS, CHIPS)).start()

    for copy in edge_copies:
        copy.wait_recv()

    with jax.named_scope("gather"):

        @pl.loop(0, 2 * own)
        def _(i):
            for h in range(HALVES):
                for b in range(STEPS):
                    perturb_g[i, h, b] = perturb_t[i, h, pl.ds(b, 8, stride=STEPS), :]

        for h in range(HALVES):
            for b in range(STEPS):
                coef_g[h, b] = coef_t[h, pl.ds(b, 8, stride=STEPS), :]

    @pl.loop(1, CHIPS)
    def _(d):
        adj_from(other_chip(d)).wait_recv()

    for f in range(FIELDS):
        for side in (0, 1):
            halo_from(f, side).wait_recv()

    with jax.named_scope("east"):
        for f in range(FIELDS):
            for h in range(HALVES):
                for b in range(STEPS):
                    adjoint_g[f, h, b] = adjoint_t[f, h, pl.ds(b, 8, stride=STEPS), :]

        @pl.loop(0, 2 * members)
        def _(k):
            i = k * FIELDS
            places = [(h, b) for h in range(HALVES) for b in range(STEPS)]
            v = {
                p: perturb_g[i, *p] * adjoint_g[0, *p] + perturb_g[i + 1, *p] * adjoint_g[1, *p]
                for p in places
            }
            for _ in range(SWEEPS):
                end = [pltpu.roll(v[h, 0], 7, 0) for h in range(HALVES)]
                flux = {
                    (h, b): coef_g[h, b] * ((v[h, b + 1] if b + 1 < STEPS else end[h]) - v[h, b])
                    for h, b in places
                }
                start = [pltpu.roll(flux[h, STEPS - 1], 1, 0) for h in range(HALVES)]
                v = {
                    (h, b): v[h, b] + flux[h, b] - (flux[h, b - 1] if b else start[h])
                    for h, b in places
                }
            for h, b in places:
                diffused[k, h, pl.ds(b, 8, stride=STEPS), :] = v[h, b]

    with jax.named_scope("turn"):
        twice = jnp.where((iota((LAT, 2 * LAT), 1) & (LAT - 1)) == iota((LAT, 2 * LAT), 0), 1.0, 0.0).astype(BF16)
        for pair in range(members):
            sides = []
            for k in (2 * pair, 2 * pair + 1):
                parts = [split(diffused[k, h, HALO : HALO + LON]) for h in range(HALVES)]
                sides.append(jnp.concatenate([p[i] for i in range(2) for p in parts], axis=1).astype(BF16))
            turned = dot(twice, jnp.concatenate(sides, axis=0), NT)
            for u in range(2):
                product[2 * pair + u] = turned[:, u * LON : (u + 1) * LON].reshape(GROUPS, 8, LANES)

    with jax.named_scope("north"):

        @pl.loop(0, 2 * members)
        def _(k):
            v = [product[k, b] for b in range(GROUPS)]
            for _ in range(SWEEPS):
                following = v[1:] + [pltpu.roll(v[0], 7, 0)]
                flux = [coef_y[b] * (following[b] - v[b]) for b in range(GROUPS)]
                before = [pltpu.roll(flux[-1], 1, 0)] + flux[:-1]
                v = [v[b] + flux[b] - before[b] for b in range(GROUPS)]
            for b in range(GROUPS):
                product[k, b] = v[b]

    share = LAT // mems

    def out_rows(c):
        return pl.ds(pl.multiple_of(c * 2 * share, 2 * share), 2 * share)

    def term_copy(to, d):
        c = other_chip(d)
        return remote(
            terms.at[to, out_rows(c)], terms_in.at[me_m], term_send.at[to, c], term_recv.at[me_m], 2 * c + to, me_t
        )

    def increments(half):
        @pl.loop(0, share, unroll=4)
        def _(b):
            at = half * share + b
            weights = [product[k, at] for k in range(2 * members)]
            for f in range(FIELDS):
                parts = [weights[k] * perturb[k * FIELDS + f, at] for k in range(2 * members)]
                while len(parts) > 1:
                    parts = [sum(parts[i : i + 2][1:], parts[i]) for i in range(0, len(parts), 2)]
                terms[half, pl.ds(2 * b + f, 8, stride=2 * share), :] = parts[0]

    with jax.named_scope("increments"):
        increments(1 - core)

    for c in order7 + [chip]:
        term_copy(1 - core, lax.rem(c - chip + CHIPS, CHIPS)).start()

    with jax.named_scope("increments"):
        increments(core)

    for c in order7:
        term_copy(core, lax.rem(c - chip + CHIPS, CHIPS)).start()

    terms_in[me_m] = terms[core, out_rows(chip)]

    @pl.loop(1, mems)
    def _(d):
        m = other_m(d)
        remote(terms_in.at[m], terms_in.at[m], term_send.at[0, 0], term_recv.at[m], sibling, me_t).wait_recv()

    for l in range(LEVELS):
        acc = terms_in[l]
        for c in range(1, CHIPS):
            acc = acc + terms_in[2 * c + l]
        out_ref[pl.ds(l, 2 * share, stride=LEVELS), :] = acc * (1.0 / (mems * members - 1))

    for copy in [to_sibling, share_copy] + edge_copies:
        copy.wait_send()

    for n in range(1, tiles):
        for to in range(2):
            list_copy(n, to).wait_send()

    @pl.loop(1, CHIPS)
    def _(d):
        part_copy(d).wait_send()
        adj_copy(d).wait_send()
        term_copy(core, d).wait_send()

    @pl.loop(0, CHIPS)
    def _(d):
        term_copy(1 - core, d).wait_send()

    for side in (0, 1):

        @pl.when(lax.rem(chip, 4) == (0 if side else 3))
        def _():
            @pl.loop(0, CHIPS)
            def _(c):
                halo_copy(c, side).wait_send()


def on_device(perturb, coef_x, coef_y, obs_values, obs_tile, obs_cell):
    tiles = lax.axis_size("tile")
    members = perturb.shape[0]
    own = members * FIELDS
    mems = 2 * CHIPS
    share = LAT // mems
    dma = pltpu.SemaphoreType.DMA

    def rows(*shape):
        return pltpu.VMEM((*shape, LANES), F32)

    out = pl.pallas_call(
        functools.partial(kernel, tiles=tiles, members=members),
        out_shape=jax.ShapeDtypeStruct((share * FIELDS * LEVELS, LANES), F32),
        in_specs=[pl.BlockSpec(memory_space=pl.ANY)] * 3 + [pl.BlockSpec(memory_space=pltpu.VMEM)] * 3,
        out_specs=pl.BlockSpec(memory_space=pltpu.VMEM),
        scratch_shapes=[
            pltpu.VMEM((own, LEVELS, LAT, LON), BF16),
            rows(LAT),
            rows(LAT),
            rows(2 * own, GROUPS, 8),
            rows(own, GROUPS, 8),
            rows(2 * own, HALVES, WIDE),
            rows(2 * own, HALVES, STEPS, 8),
            rows(HALVES, WIDE),
            rows(HALVES, STEPS, 8),
            rows(GROUPS, 8),
            rows(tiles, 8),
            rows(2 * tiles, 8),
            pltpu.VMEM((2 * FIELDS * LON, LAT), F32),
            rows(HALVES, FIELDS * LON),
            rows(CHIPS, HALVES, PART),
            rows(FIELDS, HALVES, WIDE),
            rows(FIELDS, HALVES, STEPS, 8),
            rows(2 * members, HALVES, WIDE),
            rows(2 * members, GROUPS, 8),
            rows(2, LAT),
            rows(mems, 2 * share),
            dma((4,)),
            dma((tiles, 2)), dma((2 * tiles,)),
            dma((1,)), dma((1,)),
            dma((3, 2)), dma((3, 2)),
            dma((CHIPS,)), dma((CHIPS,)),
            dma((CHIPS,)), dma((CHIPS,)),
            dma((CHIPS,)), dma((FIELDS, 2)),
            dma((2, CHIPS)), dma((mems,)),
        ],
        compiler_params=pltpu.CompilerParams(
            collective_id=0, has_side_effects=True, vmem_limit_bytes=56 * 2**20
        ),
    )(
        perturb.reshape(own, LEVELS, LAT, LON),
        coef_x,
        coef_y,
        obs_values.reshape(-1, LANES),
        obs_tile.reshape(-1, LANES),
        obs_cell.reshape(-1, LANES),
    )
    return out.reshape(share, FIELDS, LEVELS, LANES)


def solution(mesh):
    return jax.shard_map(
        on_device,
        mesh=mesh,
        in_specs=(
            P("mem", None, None, None, "tile"),
            P(None, None, "tile"),
            P(None, None, "tile"),
            P(("mem", "tile")),
            P(("mem", "tile"), None),
            P(("mem", "tile")),
        ),
        out_specs=P("mem", None, None, "tile"),
        check_vma=False,
    )
```

```python
import functools

import jax
import jax.numpy as jnp
from jax import lax
from jax.experimental import pallas as pl
from jax.experimental.pallas import tpu as pltpu
from jax.sharding import PartitionSpec as P

FIELDS = 2
LEVELS = 2
SWEEPS = 6
LAT = 256
LON = 128
CAP = 384
LANES = 128
GROUPS = LAT // 8
HALO = 8
WIDE = LON + 2 * HALO
STEPS = WIDE // 8
HALVES = LAT // LANES
CHIPS = 8
DEPTH = 8
OFFSETS = ((0, 0), (0, 1), (0, 7), (0, 2), (0, 6), (1, 0), (0, 3), (0, 5), (1, 1), (1, 7), (0, 4), (1, 2), (1, 6), (1, 3), (1, 5), (1, 4))
PART = LON // 4
F32 = jnp.float32
BF16 = jnp.bfloat16
I32 = jnp.int32
NT = (((1,), (1,)), ((), ()))
NN = (((1,), (0,)), ((), ()))


def iota(shape, dim):
    return lax.broadcasted_iota(I32, shape, dim)


def dot(a, b, dims):
    return lax.dot_general(a, b, dims, preferred_element_type=F32)


def split(x):
    high = x.astype(BF16).astype(F32)
    return high, x - high


def kernel(
    perturb_hbm, coef_x_hbm, coef_y_hbm, values_hbm, tile_hbm, cell_hbm, out_ref,
    values_ref, tile_ref, cell_ref,
    perturb_raw, coef_x_raw, coef_y_raw, perturb, perturb_out, perturb_t, perturb_g, coef_t, coef_g, coef_y,
    lists_out, lists_in, total, partial, partial_in, adjoint_t, adjoint_g, diffused, product, terms, terms_in,
    load_sem, list_send, list_recv, share_send, share_recv, edge_send, edge_recv, part_send, part_recv,
    adj_send, adj_recv, halo_send, halo_recv, term_send, term_recv,
    *, tiles, members,
):
    me_m, me_t = lax.axis_index("mem"), lax.axis_index("tile")
    chip, core = me_m // 2, lax.rem(me_m, 2)
    sibling = 2 * chip + 1 - core
    west, east = lax.rem(me_t + tiles - 1, tiles), lax.rem(me_t + 1, tiles)
    blocks = values_ref.shape[0]
    mems = 2 * CHIPS
    own = members * FIELDS

    def remote(src, dst, send, recv, m, t):
        return pltpu.make_async_remote_copy(
            src_ref=src, dst_ref=dst, send_sem=send, recv_sem=recv,
            device_id={"mem": m, "tile": t}, device_id_type=pl.DeviceIdType.MESH,
        )

    def signal(m, t):
        pl.semaphore_signal(
            barrier, 1, device_id={"mem": m, "tile": t}, device_id_type=pl.DeviceIdType.MESH
        )

    def other_chip(d):
        return lax.rem(chip + d, CHIPS)

    order7 = [lax.rem(chip // 4 + y, 2) * 4 + lax.rem(lax.rem(chip, 4) + x, 4) for y, x in ((1, 2), (1, 1), (1, 3), (0, 2), (1, 0), (0, 1), (0, 3))]

    def other_m(d):
        return lax.rem(me_m + d, mems)

    loads = [
        pltpu.make_async_copy(src, dst, load_sem.at[i])
        for i, (src, dst) in enumerate(
            (
                (perturb_hbm.at[:, 1 - core], perturb_raw.at[:, 1 - core]),
                (perturb_hbm.at[:, core], perturb_raw.at[:, core]),
                (coef_x_hbm.at[core], coef_x_raw),
                (coef_y_hbm.at[core], coef_y_raw),
                (tile_hbm, tile_ref),
                (values_hbm, values_ref),
                (cell_hbm, cell_ref),
            )
        )
    ]

    barrier = pltpu.get_barrier_semaphore()
    signal(sibling, me_t)

    @pl.loop(1, tiles)
    def _(d):
        t = lax.rem(me_t + d, tiles)
        signal(me_m, t)
        signal(sibling, t)

    @pl.loop(1, CHIPS)
    def _(d):
        m = 2 * other_chip(d) + core
        signal(m, me_t)
        signal(2 * other_chip(d) + 1 - core, me_t)
        signal(m, west)
        signal(m, east)

    for copy in loads[4:] + loads[:4]:
        copy.start()
    for copy in loads[4:]:
        copy.wait()

    with jax.named_scope("bucket"):
        tile = tile_ref[...]
        hot = jnp.concatenate([jnp.where(tile == t, 1.0, 0.0) for t in range(tiles)], axis=0)
        hot16 = hot.astype(BF16)
        lane_r, lane_c = iota((LANES, 2 * LANES), 0), iota((LANES, 2 * LANES), 1)
        earlier = jnp.where((lane_r < lane_c) | (lane_c >= LANES), 1.0, 0.0).astype(BF16)
        counts = dot(hot16, earlier, NN)
        rows = tiles * blocks
        row, col = iota((rows, rows), 0), iota((rows, rows), 1)
        before = (row // blocks == col // blocks) & (col < row)
        base = dot(jnp.where(before, 1.0, 0.0).astype(BF16), counts[:, LANES:].astype(BF16), NN)
        ranks = hot * (counts[:, :LANES] + base)
        rank = ranks[0:blocks]
        for t in range(1, tiles):
            rank = rank + ranks[t * blocks : (t + 1) * blocks]
        rank = rank.astype(I32)
        slot_row, slot_lane = tile * 8 + (rank >> 7), rank & 127
        cell = cell_ref[...]
        value_parts = split(values_ref[...])
        cell_parts = [(cell & mask).astype(F32) for mask in (0x7F, 0x7F << 7, 0x7 << 14)]
        sums = None
        for start in range(0, blocks, 4):
            left, right = [], []
            for b in range(start, start + 4):
                at = iota((8 * tiles, LANES), 0)
                here = at == slot_row[b : b + 1]
                there = at == slot_row[b : b + 1] + 3
                left.append(
                    jnp.concatenate(
                        [jnp.where(here, part[b : b + 1], 0.0) for part in value_parts]
                        + [jnp.where(there, part[b : b + 1], 0.0) for part in cell_parts],
                        axis=0,
                    ).astype(BF16)
                )
                right.append(jnp.where(iota((LANES, LANES), 0) == slot_lane[b : b + 1], 1.0, 0.0).astype(BF16))
            got = dot(jnp.concatenate(left, axis=1), jnp.concatenate(right, axis=1), NT)
            sums = got if sums is None else sums + got
        packed = sums[0 : 8 * tiles]
        for i in range(1, 5):
            packed = packed + sums[8 * tiles * i : 8 * tiles * (i + 1)]
        lists_out[...] = packed.reshape(tiles, 8, LANES)
    pl.semaphore_wait(barrier, 1 + 2 * (tiles - 1) + 4 * (CHIPS - 1))

    def list_copy(n, to):
        y, z = OFFSETS[n]
        t = lax.rem(me_t // DEPTH + y, 2) * DEPTH + lax.rem(me_t + DEPTH - z, DEPTH)
        return remote(
            lists_out.at[t], lists_in.at[2 * n + core], list_send.at[n, to], list_recv.at[2 * n + core],
            2 * chip + to, t,
        )

    to_sibling = remote(
        lists_out.at[me_t], lists_in.at[core], list_send.at[0, 0], list_recv.at[core], sibling, me_t
    )
    for n in range(tiles - 1, 0, -1):
        for to in range(2):
            list_copy(n, to).start()
    to_sibling.start()
    lists_in[core] = lists_out[me_t]

    to, source = iota((LAT, LAT), 0), iota((LAT, LAT), 1)
    order = jnp.where(source == (to % 8) * GROUPS + to // 8, 1.0, 0.0).astype(BF16)
    same = jnp.where(iota((LON, LON), 0) == iota((LON, LON), 1), 1.0, 0.0).astype(BF16)

    def ordered(l, f):
        side = jnp.concatenate([perturb_raw[k * FIELDS + f, l] for k in range(members)], axis=1)
        got = dot(order, side, NN)
        return [got[:, k * LON : (k + 1) * LON] for k in range(members)]

    def turn_in(i, x):
        turned = dot(same, x.astype(BF16), NT)
        for h in range(HALVES):
            perturb_t[i, h, HALO : HALO + LON] = turned[:, h * LANES : (h + 1) * LANES]

    share_copy = remote(perturb_out, perturb.at[pl.ds(own, own)], share_send.at[0], share_recv.at[0], sibling, me_t)
    loads[0].wait()
    with jax.named_scope("share"):
        for f in range(FIELDS):
            for k, x in enumerate(ordered(1 - core, f)):
                perturb_out[k * FIELDS + f] = x.reshape(GROUPS, 8, LANES)
    share_copy.start()
    for copy in loads[1:4]:
        copy.wait()
    with jax.named_scope("prepare"):
        for f in range(FIELDS):
            for k, x in enumerate(ordered(core, f)):
                perturb[k * FIELDS + f] = x.reshape(GROUPS, 8, LANES)
                turn_in(k * FIELDS + f, x)
        faces = []
        for b in range(GROUPS):
            faces.append(coef_x_raw[pl.ds(b, 8, stride=GROUPS), :])
            face = coef_y_raw[pl.ds(b, 8, stride=GROUPS), :]
            if b == GROUPS - 1:
                face = jnp.where(iota((8, LANES), 0) < 7, face, 0.0)
            coef_y[b] = face
        faces = jnp.concatenate(faces, axis=0)
        for h in range(HALVES):
            coef_t[h, HALO : HALO + LON] = faces[h * LANES : (h + 1) * LANES].T

    def edges_of(start):
        mine, theirs = pl.ds(0, own), pl.ds(own, own)
        at = pl.ds(start, HALO)
        return coef_t.at[:, at], perturb_t.at[mine, :, at], perturb_t.at[theirs, :, at]

    edge_copies = []
    for i in range(3):
        edge_copies.append(
            remote(edges_of(LON)[i], edges_of(0)[i], edge_send.at[i, 0], edge_recv.at[i, 0], me_m, east)
        )
        edge_copies.append(
            remote(edges_of(HALO)[i], edges_of(HALO + LON)[i], edge_send.at[i, 1], edge_recv.at[i, 1], me_m, west)
        )
    for copy in edge_copies[:4]:
        copy.start()

    share_copy.wait_recv()
    with jax.named_scope("prepare"):
        for i in range(own, 2 * own):
            turn_in(i, perturb[i].reshape(LAT, LANES))

    for copy in edge_copies[4:]:
        copy.start()

    def rows(c):
        return pl.ds(pl.multiple_of(c * PART, PART), PART)

    def part_copy(d):
        c = other_chip(d)
        return remote(
            partial.at[:, rows(c)], partial_in.at[chip], part_send.at[d], part_recv.at[d], 2 * c + core, me_t
        )

    with jax.named_scope("deposit"):
        per_list = CAP // LANES
        span = 8
        counting = (iota((LAT // 16, 16, LANES), 0) * 16 + iota((LAT // 16, 16, LANES), 1)).astype(F32).astype(BF16)
        one, zero = jnp.ones((), BF16), jnp.zeros((), BF16)

        def repeated(x):
            return jnp.broadcast_to(x, (16, LANES)).astype(BF16)[None]

        @pl.loop(0, FIELDS)
        def _(turn):
            f = lax.rem(1 - chip // 4 + turn, 2)
            total[...] = jnp.zeros_like(total)

            @pl.loop(0, tiles // span)
            def _(i):
                for n in range(2 * span):
                    at = i * 2 * span + n

                    @pl.when((turn == 0) & (at != core))
                    def _():
                        remote(
                            lists_out.at[0], lists_in.at[at], list_send.at[0, 0], list_recv.at[at], sibling, me_t
                        ).wait_recv()

                lists = lists_in[pl.ds(i * 2 * span, 2 * span)]
                cells = lists.astype(I32)
                channel = cells >> 15
                grid_row = (((channel & 1) ^ core) << 10) | ((channel >> 1) << 7) | (cells & (LON - 1))
                grid_row = (grid_row - f * LON).astype(F32)
                grid_lane = (cells >> 7) & (LAT - 1)
                grid_lane = (((grid_lane & (GROUPS - 1)) << 3) | (grid_lane >> 5)).astype(F32)
                parts = split(lists)
                left, right = [], []
                for u in range(2 * span):
                    for j in range(per_list):
                        here = counting == repeated(grid_lane[u, 3 + j : 4 + j])
                        right.append(jnp.where(here, one, zero).reshape(LAT, LANES))
                        here = counting[: LON // 16] == repeated(grid_row[u, 3 + j : 4 + j])
                        left.append(
                            jnp.concatenate(
                                [
                                    jnp.where(here, repeated(part[u, j : j + 1]), zero).reshape(LON, LANES)
                                    for part in parts
                                ],
                                axis=0,
                            )
                        )
                total[...] += dot(jnp.concatenate(left, axis=1), jnp.concatenate(right, axis=1), NT)

            for h in range(HALVES):
                lanes = slice(h * LANES, (h + 1) * LANES)
                partial[h, pl.ds(pl.multiple_of(f * LON, LON), LON)] = total[:LON, lanes] + total[LON:, lanes]
            for x in (2, 1, 3, 0):
                c = f * 4 + lax.rem(lax.rem(chip, 4) + x, 4)

                @pl.when(c != chip)
                def _():
                    part_copy(lax.rem(c - chip + CHIPS, CHIPS)).start()

    def block(c):
        start = pl.multiple_of(HALO + lax.rem(c, 4) * PART, 8)
        return adjoint_t.at[c // 4, :, pl.ds(start, PART)]

    def add_part(d, acc):
        part_copy(d).wait_recv()
        return acc + partial_in[other_chip(CHIPS - d)]

    block(chip)[...] = lax.fori_loop(1, CHIPS, add_part, partial[:, rows(chip)])

    def adj_copy(d):
        mine = block(chip)
        return remote(mine, mine, adj_send.at[d], adj_recv.at[chip], 2 * other_chip(d) + core, me_t)

    def adj_from(c):
        there = block(c)
        return remote(there, there, adj_send.at[0], adj_recv.at[c], 2 * other_chip(1) + core, me_t)

    def halo_at(f, start):
        return adjoint_t.at[f, :, pl.ds(start, HALO)]

    def halo_copy(c, side):
        f = chip // 4
        source = halo_at(f, HALO if side else LON)
        target = halo_at(f, HALO + LON if side else 0)
        return remote(
            source, target, halo_send.at[c], halo_recv.at[f, side], 2 * c + core, west if side else east
        )

    def halo_from(f, side):
        target = halo_at(f, HALO + LON if side else 0)
        return remote(target, target, halo_send.at[0], halo_recv.at[f, side], me_m, east)

    for side in (0, 1):

        @pl.when(lax.rem(chip, 4) == (0 if side else 3))
        def _():
            @pl.loop(0, CHIPS)
            def _(c):
                halo_copy(c, side).start()

    for c in order7:
        adj_copy(lax.rem(c - chip + CHIPS, CHIPS)).start()

    for copy in edge_copies:
        copy.wait_recv()

    with jax.named_scope("gather"):

        @pl.loop(0, 2 * own)
        def _(i):
            for h in range(HALVES):
                for b in range(STEPS):
                    perturb_g[i, h, b] = perturb_t[i, h, pl.ds(b, 8, stride=STEPS), :]

        for h in range(HALVES):
            for b in range(STEPS):
                coef_g[h, b] = coef_t[h, pl.ds(b, 8, stride=STEPS), :]

    @pl.loop(1, CHIPS)
    def _(d):
        adj_from(other_chip(d)).wait_recv()

    for f in range(FIELDS):
        for side in (0, 1):
            halo_from(f, side).wait_recv()

    with jax.named_scope("east"):
        for f in range(FIELDS):
            for h in range(HALVES):
                for b in range(STEPS):
                    adjoint_g[f, h, b] = adjoint_t[f, h, pl.ds(b, 8, stride=STEPS), :]

        @pl.loop(0, 2 * members)
        def _(k):
            i = k * FIELDS
            places = [(h, b) for h in range(HALVES) for b in range(STEPS)]
            v = {
                p: perturb_g[i, *p] * adjoint_g[0, *p] + perturb_g[i + 1, *p] * adjoint_g[1, *p]
                for p in places
            }
            for _ in range(SWEEPS):
                end = [pltpu.roll(v[h, 0], 7, 0) for h in range(HALVES)]
                flux = {
                    (h, b): coef_g[h, b] * ((v[h, b + 1] if b + 1 < STEPS else end[h]) - v[h, b])
                    for h, b in places
                }
                start = [pltpu.roll(flux[h, STEPS - 1], 1, 0) for h in range(HALVES)]
                v = {
                    (h, b): v[h, b] + flux[h, b] - (flux[h, b - 1] if b else start[h])
                    for h, b in places
                }
            for h, b in places:
                diffused[k, h, pl.ds(b, 8, stride=STEPS), :] = v[h, b]

    with jax.named_scope("turn"):
        twice = jnp.where((iota((LAT, 2 * LAT), 1) & (LAT - 1)) == iota((LAT, 2 * LAT), 0), 1.0, 0.0).astype(BF16)
        for pair in range(members):
            sides = []
            for k in (2 * pair, 2 * pair + 1):
                parts = [split(diffused[k, h, HALO : HALO + LON]) for h in range(HALVES)]
                sides.append(jnp.concatenate([p[i] for i in range(2) for p in parts], axis=1).astype(BF16))
            turned = dot(twice, jnp.concatenate(sides, axis=0), NT)
            for u in range(2):
                product[2 * pair + u] = turned[:, u * LON : (u + 1) * LON].reshape(GROUPS, 8, LANES)

    with jax.named_scope("north"):

        @pl.loop(0, 2 * members)
        def _(k):
            v = [product[k, b] for b in range(GROUPS)]
            for _ in range(SWEEPS):
                following = v[1:] + [pltpu.roll(v[0], 7, 0)]
                flux = [coef_y[b] * (following[b] - v[b]) for b in range(GROUPS)]
                before = [pltpu.roll(flux[-1], 1, 0)] + flux[:-1]
                v = [v[b] + flux[b] - before[b] for b in range(GROUPS)]
            for b in range(GROUPS):
                product[k, b] = v[b]

    share = LAT // mems

    def out_rows(c):
        return pl.ds(pl.multiple_of(c * 2 * share, 2 * share), 2 * share)

    def term_copy(to, d):
        c = other_chip(d)
        return remote(
            terms.at[to, out_rows(c)], terms_in.at[me_m], term_send.at[to, c], term_recv.at[me_m], 2 * c + to, me_t
        )

    def increments(half):
        @pl.loop(0, share, unroll=4)
        def _(b):
            at = half * share + b
            weights = [product[k, at] for k in range(2 * members)]
            for f in range(FIELDS):
                parts = [weights[k] * perturb[k * FIELDS + f, at] for k in range(2 * members)]
                while len(parts) > 1:
                    parts = [sum(parts[i : i + 2][1:], parts[i]) for i in range(0, len(parts), 2)]
                terms[half, pl.ds(2 * b + f, 8, stride=2 * share), :] = parts[0]

    with jax.named_scope("increments"):
        increments(1 - core)

    for c in order7 + [chip]:
        term_copy(1 - core, lax.rem(c - chip + CHIPS, CHIPS)).start()

    with jax.named_scope("increments"):
        increments(core)

    for c in order7:
        term_copy(core, lax.rem(c - chip + CHIPS, CHIPS)).start()

    terms_in[me_m] = terms[core, out_rows(chip)]

    @pl.loop(1, mems)
    def _(d):
        m = other_m(d)
        remote(terms_in.at[m], terms_in.at[m], term_send.at[0, 0], term_recv.at[m], sibling, me_t).wait_recv()

    for l in range(LEVELS):
        acc = terms_in[l]
        for c in range(1, CHIPS):
            acc = acc + terms_in[2 * c + l]
        out_ref[pl.ds(l, 2 * share, stride=LEVELS), :] = acc * (1.0 / (mems * members - 1))

    for copy in [to_sibling, share_copy] + edge_copies:
        copy.wait_send()

    for n in range(1, tiles):
        for to in range(2):
            list_copy(n, to).wait_send()

    @pl.loop(1, CHIPS)
    def _(d):
        part_copy(d).wait_send()
        adj_copy(d).wait_send()
        term_copy(core, d).wait_send()

    @pl.loop(0, CHIPS)
    def _(d):
        term_copy(1 - core, d).wait_send()

    for side in (0, 1):

        @pl.when(lax.rem(chip, 4) == (0 if side else 3))
        def _():
            @pl.loop(0, CHIPS)
            def _(c):
                halo_copy(c, side).wait_send()


def on_device(perturb, coef_x, coef_y, obs_values, obs_tile, obs_cell):
    tiles = lax.axis_size("tile")
    members = perturb.shape[0]
    own = members * FIELDS
    mems = 2 * CHIPS
    share = LAT // mems
    blocks = obs_values.shape[0] // LANES
    dma = pltpu.SemaphoreType.DMA

    def rows(*shape):
        return pltpu.VMEM((*shape, LANES), F32)

    out = pl.pallas_call(
        functools.partial(kernel, tiles=tiles, members=members),
        out_shape=jax.ShapeDtypeStruct((share * FIELDS * LEVELS, LANES), F32),
        in_specs=[pl.BlockSpec(memory_space=pl.ANY)] * 6,
        out_specs=pl.BlockSpec(memory_space=pltpu.VMEM),
        scratch_shapes=[
            pltpu.VMEM((blocks, LANES), F32),
            pltpu.VMEM((blocks, LANES), I32),
            pltpu.VMEM((blocks, LANES), I32),
            pltpu.VMEM((own, LEVELS, LAT, LON), BF16),
            rows(LAT),
            rows(LAT),
            rows(2 * own, GROUPS, 8),
            rows(own, GROUPS, 8),
            rows(2 * own, HALVES, WIDE),
            rows(2 * own, HALVES, STEPS, 8),
            rows(HALVES, WIDE),
            rows(HALVES, STEPS, 8),
            rows(GROUPS, 8),
            rows(tiles, 8),
            rows(2 * tiles, 8),
            pltpu.VMEM((2 * LON, LAT), F32),
            rows(HALVES, FIELDS * LON),
            rows(CHIPS, HALVES, PART),
            rows(FIELDS, HALVES, WIDE),
            rows(FIELDS, HALVES, STEPS, 8),
            rows(2 * members, HALVES, WIDE),
            rows(2 * members, GROUPS, 8),
            rows(2, LAT),
            rows(mems, 2 * share),
            dma((7,)),
            dma((tiles, 2)), dma((2 * tiles,)),
            dma((1,)), dma((1,)),
            dma((3, 2)), dma((3, 2)),
            dma((CHIPS,)), dma((CHIPS,)),
            dma((CHIPS,)), dma((CHIPS,)),
            dma((CHIPS,)), dma((FIELDS, 2)),
            dma((2, CHIPS)), dma((mems,)),
        ],
        compiler_params=pltpu.CompilerParams(
            collective_id=0, has_side_effects=True, vmem_limit_bytes=56 * 2**20
        ),
    )(
        perturb.reshape(own, LEVELS, LAT, LON),
        coef_x,
        coef_y,
        obs_values.reshape(-1, LANES),
        obs_tile.reshape(-1, LANES),
        obs_cell.reshape(-1, LANES),
    )
    return out.reshape(share, FIELDS, LEVELS, LANES)


def solution(mesh):
    return jax.shard_map(
        on_device,
        mesh=mesh,
        in_specs=(
            P("mem", None, None, None, "tile"),
            P(None, None, "tile"),
            P(None, None, "tile"),
            P(("mem", "tile")),
            P(("mem", "tile"), None),
            P(("mem", "tile")),
        ),
        out_specs=P("mem", None, None, "tile"),
        check_vma=False,
    )
```
